128 devices in a mesh: row: 8 (over x, y_hi), col: 16 (over y_lo, z, core).
Axes of the slice: x: 4, y: 4 (y_hi: 2, y_lo: 2; y = y_hi * 2 + y_lo), z: 4, core: 2. Of those that a mesh axis runs over, the one named last changes fastest.
Arguments:
- coupling: bfloat16 [32768, 32768], P('row', 'col'), may hold values from -0.03125 to 0.03125
- amplitude: float32 [64, 32768], P(None, 'col'), may hold values from -0.95 to 0.95
- target: float32 [64, 32768], P(None, 'col'), may hold values from -6 to 6
- shadow_target: float32 [64, 32768], P(None, 'col'), may hold values from -10.2 to 10.2
Outputs:
- solution: float32 [64, 32768], P(None, 'col')
- shadow_solution: float32 [64, 32768], P(None, 'col')
- residual: float32 [64, 32768], P(None, 'col')
- shadow_residual: float32 [64, 32768], P(None, 'col')
The draws below stay inside these ranges and needn't reach their ends.
All inputs are finite; a program needn't handle non-finite values.
Results may differ from the reference program's by a relative error of at most 0.0036.
Values may be sent and summed in bfloat16 or wider, within the bound.
No kernel may reach another device: no remote copies, remote signals or barrier semaphores. Data moves between devices by JAX's collectives and lax.ppermute only.
A program may use at most 128 MiB of HBM per device.

```python
import jax
import jax.numpy as jnp
from jax import lax

REPS = 64
ITERS = 2
N = 32768


def source_values(key):
    fresh_key = jax.random.fold_in(key, 7)
    return jnp.clip(jax.random.normal(fresh_key, (REPS, N), jnp.float32), -6.0, 6.0)


def draw_target(key, part):
    return source_values(key)


def draw_shadow_target(key, part):
    factor = jax.random.uniform(jax.random.fold_in(key, 11), (REPS, N), jnp.float32, 0.3, 1.7)
    return source_values(key) * factor


def level_of(stream_key, shape, pieces, smallest, high):
    loudness, own = 1.0, jax.random.fold_in(stream_key, 6)
    for axis_at, parts in pieces:
        steps = jnp.exp(jax.random.uniform(jax.random.fold_in(own, axis_at), (parts,), jnp.float32, smallest / len(pieces), high / len(pieces)))
        loudness = loudness * jnp.repeat(steps, shape[axis_at] // parts).reshape([-1 if axis == axis_at else 1 for axis in range(len(shape))])
    return loudness


def centred(stream_key, dims, deviation, bound, pieces=(), held_as=jnp.bfloat16):
    level = level_of(stream_key, dims, pieces, -0.22, 0.18) if pieces else 1.0
    drawn = jax.random.normal(stream_key, dims, jnp.float32) * deviation * level
    return jnp.minimum(jnp.maximum(drawn, -bound), bound).astype(held_as)


def setup_inputs(seed: int = 0) -> dict:
    arg_keys = jax.random.split(jax.random.key(seed), 5)
    coupling = centred(arg_keys[0], (N, N), N ** -0.5, 0.03125, ((0, 8), (1, 16)))
    amplitude = jnp.clip(jax.random.uniform(arg_keys[1], (REPS, N), jnp.float32, -0.95, 0.95) * level_of(arg_keys[1], (REPS, N), ((1, 16),), -0.4, 0.0), -0.95, 0.95)
    target = draw_target(jax.random.fold_in(arg_keys[4], 71), 0)
    shadow_target = draw_shadow_target(jax.random.fold_in(arg_keys[4], 71), 0)
    return dict(coupling=coupling, amplitude=amplitude, target=target, shadow_target=shadow_target)


SELF_GAIN = 0.5
COUPLE_GAIN = 0.3


def reference(coupling, amplitude, target, shadow_target):
    slope = 1.0 - amplitude * amplitude
    solution = jnp.zeros_like(target)
    shadow_solution = jnp.zeros_like(target)
    residual = target
    shadow_residual = shadow_target
    direction = target
    shadow_direction = shadow_target
    align = jnp.sum(shadow_residual * residual, axis=1)
    for iteration in range(ITERS):
        scaled = (slope * direction).astype(jnp.bfloat16)
        product = jnp.dot(scaled, coupling, preferred_element_type=jnp.float32)
        image = direction - SELF_GAIN * slope * direction - COUPLE_GAIN * product
        shadow_scaled = shadow_direction.astype(jnp.bfloat16)
        shadow_product = lax.dot_general(shadow_scaled, coupling, (((1,), (1,)), ((), ())), preferred_element_type=jnp.float32)
        shadow_image = shadow_direction - SELF_GAIN * slope * shadow_direction - COUPLE_GAIN * slope * shadow_product
        curve = jnp.sum(shadow_direction * image, axis=1)
        step_size = (align / curve)[:, None]
        solution = solution + step_size * direction
        shadow_solution = shadow_solution + step_size * shadow_direction
        residual = residual - step_size * image
        shadow_residual = shadow_residual - step_size * shadow_image
        if iteration + 1 < ITERS:
            align_next = jnp.sum(shadow_residual * residual, axis=1)
            blend = (align_next / align)[:, None]
            direction = residual + blend * direction
            shadow_direction = shadow_residual + blend * shadow_direction
            align = align_next
    return solution, shadow_solution, residual, shadow_residual
```

```python
import jax
import jax.numpy as jnp
from jax import lax
from jax.sharding import PartitionSpec as P

SELF_GAIN = 0.5
COUPLE_GAIN = 0.3

F32 = jnp.float32
BF16 = jnp.bfloat16
WIRE = jnp.float16
AXES = ("row", "col")

FIRST_SCALE = 32.0
SECOND_SCALE = 1.0 / 16.0


def split(d):
    row, col = divmod(d, 16)
    return row // 2, row % 2, col // 8, (col // 2) % 4, col % 2


def join(x, yh, yl, z, h):
    return (x * 2 + yh) * 16 + yl * 8 + z * 2 + h


def sends(source_of):
    return [(join(*source_of(*split(d))), d) for d in range(128)]


def flip_x(x, yh, yl, z, h):
    return x ^ 1, yh, yl, z, h


def mirror_x(x, yh, yl, z, h):
    return 3 - x, yh, yl, z, h


def flip_yh(x, yh, yl, z, h):
    return x, yh ^ 1, yl, z, h


def flip_yl(x, yh, yl, z, h):
    return x, yh, yl ^ 1, z, h


def flip_z(x, yh, yl, z, h):
    return x, yh, yl, z ^ 1, h


def mirror_z(x, yh, yl, z, h):
    return x, yh, yl, 3 - z, h


def flip_core(x, yh, yl, z, h):
    return x, yh, yl, z, h ^ 1


def by_core(first, second):
    return sends(lambda *d: (second if d[4] else first)(*d))


STEP = ({0: 2, 1: 1, 2: 0, 3: 3}, {0: 2, 1: 3, 2: 0, 3: 1})


def from_rows(x, yh, yl, z, h):
    xs, yhs = 2 * yl + z // 2, z % 2
    return xs, yhs, yl ^ yh ^ yhs, (z + STEP[h][(x - xs) % 4]) % 4, h


def from_cols(x, yh, yl, z, h):
    yls, zs = x // 2, (x % 2) * 2 + yh
    return (x + STEP[h][(z - zs) % 4]) % 4, yh ^ yl ^ yls, yls, zs, h


CORE = sends(flip_core)
TO_COLS = sends(from_rows)
TO_ROWS = sends(from_cols)
ROW_STEPS = (
    by_core(flip_x, flip_yh),
    by_core(mirror_x, flip_x),
    by_core(flip_yh, mirror_x),
)
COL_STEPS = (
    by_core(flip_yl, flip_z),
    by_core(flip_z, mirror_z),
    by_core(mirror_z, flip_yl),
)
SMALL_COL = (CORE, sends(flip_yl), sends(flip_z), sends(mirror_z))


def move(value, pairs):
    return lax.ppermute(value, AXES, pairs)


def chip_sum(value, steps):
    for pairs in steps:
        held = value.astype(WIRE)
        value = held.astype(F32) + move(held, pairs).astype(F32)
    return value


def on_device(coupling, amplitude, target, shadow_target):
    core = lax.axis_index("col") % 2
    first = core == 0
    g, gs = target, shadow_target
    slope = 1.0 - amplitude * amplitude
    keep = 1.0 - SELF_GAIN * slope

    tops = jnp.stack([jnp.max(jnp.abs(g), axis=1), jnp.max(jnp.abs(gs), axis=1)])
    sums = jnp.stack([jnp.sum(gs * g, axis=1), jnp.sum(gs * (keep * g), axis=1)])
    stats = jnp.concatenate([tops, sums])
    for pairs in SMALL_COL:
        other = move(stats, pairs)
        stats = jnp.concatenate(
            [jnp.maximum(stats[:2], other[:2]), stats[2:] + other[2:]]
        )
    tiny = 1e-30
    top = jnp.maximum(stats[0], tiny)[:, None]
    shadow_top = jnp.maximum(stats[1], tiny)[:, None]
    align = stats[2]
    alpha = jnp.clip(stats[2] / stats[3], 1.0, 2.05)
    alpha = jnp.where(jnp.isnan(alpha), 1.4, alpha)
    alpha_c = alpha[:, None]

    def rows_of(vector):
        scaled = (slope * vector).astype(BF16)
        mine = move(scaled, TO_ROWS)
        other = move(mine, CORE)
        low = jnp.where(first, mine, other)
        high = jnp.where(first, other, mine)
        return jnp.concatenate([low, high], axis=1)

    def primary(row_block):
        return jnp.dot(row_block, coupling, preferred_element_type=F32)

    def shadow(vector):
        return lax.dot_general(
            vector.astype(BF16),
            coupling,
            (((1,), (1,)), ((), ())),
            preferred_element_type=F32,
        )

    def primary_sum(partial, scale):
        return chip_sum(partial * scale, ROW_STEPS) * (1.0 / scale)

    def shadow_sum(partial, scale):
        low, high = partial[:, :2048] * scale, partial[:, 2048:] * scale
        mine = jnp.where(first, low, high)
        other = jnp.where(first, high, low).astype(WIRE)
        mine = mine + move(other, CORE).astype(F32)
        total = chip_sum(mine, COL_STEPS).astype(WIRE)
        return move(total, TO_COLS).astype(F32) * (1.0 / scale)

    shadow_partial = shadow(gs)
    primary_partial = primary(rows_of(g))
    product = primary_sum(primary_partial, FIRST_SCALE / top)
    shadow_product = shadow_sum(shadow_partial, FIRST_SCALE / shadow_top)
    p1 = keep * g - COUPLE_GAIN * product
    q1 = keep * gs - COUPLE_GAIN * slope * shadow_product
    u = g - alpha_c * p1
    us = gs - alpha_c * q1

    shadow_partial = shadow(us)
    primary_partial = primary(rows_of(u))
    product = primary_sum(primary_partial, SECOND_SCALE / top)
    shadow_product = shadow_sum(shadow_partial, SECOND_SCALE / shadow_top)
    p2 = keep * u - COUPLE_GAIN * product
    q2 = keep * us - COUPLE_GAIN * slope * shadow_product

    dots = jnp.stack(
        [
            jnp.sum(gs * p1, axis=1),
            jnp.sum(us * g, axis=1),
            jnp.sum(gs * u, axis=1),
            jnp.sum(us * u, axis=1),
            jnp.sum(us * p1, axis=1),
            jnp.sum(q1 * u, axis=1),
            jnp.sum(us * p2, axis=1),
        ]
    )
    for pairs in SMALL_COL:
        dots = dots + move(dots, pairs)
    curve, us_g, gs_u, us_u, us_p1, q1_u, us_p2 = (dots[i] for i in range(7))
    step = align / curve
    kappa = step / alpha
    rest = 1.0 - kappa
    align_next = rest * rest * align + kappa * rest * (us_g + gs_u) + kappa * kappa * us_u
    blend = align_next / align
    lead = rest + blend
    curve_next = (
        lead * lead * curve + lead * kappa * (us_p1 + q1_u) + kappa * kappa * us_p2
    )
    step_next = align_next / curve_next

    def column(value):
        return value[:, None]

    step, kappa, lead, step_next = map(column, (step, kappa, lead, step_next))
    direction = lead * g + kappa * u
    shadow_direction = lead * gs + kappa * us
    solution = step * g + step_next * direction
    shadow_solution = step * gs + step_next * shadow_direction
    residual = g - step * p1 - step_next * (lead * p1 + kappa * p2)
    shadow_residual = gs - step * q1 - step_next * (lead * q1 + kappa * q2)
    return (solution, shadow_solution, residual, shadow_residual)


def solution(mesh):
    return jax.shard_map(
        on_device,
        mesh=mesh,
        in_specs=(P("row", "col"), P(None, "col"), P(None, "col"), P(None, "col")),
        out_specs=(P(None, "col"), P(None, "col"), P(None, "col"), P(None, "col")),
        check_vma=False,
    )
```

```python
import jax
import jax.numpy as jnp
from jax import lax
from jax.experimental import pallas as pl
from jax.experimental.pallas import tpu as pltpu
from jax.sharding import PartitionSpec as P

SELF_GAIN = 0.5
COUPLE_GAIN = 0.3

F32 = jnp.float32
BF16 = jnp.bfloat16
WIRE = jnp.float16
AXES = ("row", "col")

FIRST_SCALE = 32.0
SECOND_SCALE = 1.0 / 16.0


def split(d):
    row, col = divmod(d, 16)
    return row // 2, row % 2, col // 8, (col // 2) % 4, col % 2


def join(x, yh, yl, z, h):
    return (x * 2 + yh) * 16 + yl * 8 + z * 2 + h


def sends(source_of):
    return [(join(*source_of(*split(d))), d) for d in range(128)]


def flip_x(x, yh, yl, z, h):
    return x ^ 1, yh, yl, z, h


def mirror_x(x, yh, yl, z, h):
    return 3 - x, yh, yl, z, h


def flip_yh(x, yh, yl, z, h):
    return x, yh ^ 1, yl, z, h


def flip_yl(x, yh, yl, z, h):
    return x, yh, yl ^ 1, z, h


def flip_z(x, yh, yl, z, h):
    return x, yh, yl, z ^ 1, h


def mirror_z(x, yh, yl, z, h):
    return x, yh, yl, 3 - z, h


def flip_core(x, yh, yl, z, h):
    return x, yh, yl, z, h ^ 1


def by_core(first, second):
    return sends(lambda *d: (second if d[4] else first)(*d))


STEP = ({0: 2, 1: 1, 2: 0, 3: 3}, {0: 2, 1: 3, 2: 0, 3: 1})


def from_rows(x, yh, yl, z, h):
    xs, yhs = 2 * yl + z // 2, z % 2
    return xs, yhs, yl ^ yh ^ yhs, (z + STEP[h][(x - xs) % 4]) % 4, h


def from_cols(x, yh, yl, z, h):
    yls, zs = x // 2, (x % 2) * 2 + yh
    return (x + STEP[h][(z - zs) % 4]) % 4, yh ^ yl ^ yls, yls, zs, h


HALF_SOURCE = (
    7, 4, 3, 7, 0, 2, 4, 1, 6, 6, 2, 3, 1, 0, 5, 5,
    7, 0, 2, 5, 0, 6, 5, 7, 6, 2, 4, 3, 1, 4, 3, 1,
    6, 0, 4, 1, 1, 6, 3, 3, 0, 2, 2, 7, 7, 4, 5, 5,
    0, 4, 5, 1, 7, 2, 2, 7, 1, 0, 3, 3, 6, 6, 4, 5,
    0, 6, 3, 7, 7, 4, 4, 1, 1, 0, 5, 3, 6, 2, 2, 5,
    7, 2, 3, 7, 0, 0, 4, 5, 1, 6, 2, 1, 6, 4, 5, 3,
    6, 6, 4, 3, 1, 0, 3, 5, 0, 4, 5, 7, 7, 2, 2, 1,
    0, 4, 5, 7, 7, 2, 2, 1, 6, 0, 3, 5, 1, 6, 4, 3,
)

CORE = sends(flip_core)
TO_COLS = sends(from_rows)
TO_ROWS = sends(from_cols)
HALF_TO_ROWS = [
    (HALF_SOURCE[d] * 16 + (d // 16) * 2 + d % 2, d) for d in range(128)
]
ROW_STEPS = (
    by_core(flip_x, flip_yh),
    by_core(mirror_x, flip_x),
    by_core(flip_yh, mirror_x),
)
COL_STEPS = (
    by_core(flip_yl, flip_z),
    by_core(flip_z, mirror_z),
    by_core(mirror_z, flip_yl),
)
Z_PAIR = sends(flip_z)
SMALL_COL = (CORE, sends(flip_yl), sends(flip_z), sends(mirror_z))
SMALL_ROW = (CORE, sends(flip_x), sends(mirror_x), sends(flip_yh))

TILE = 512


def primary_kernel(left_ref, coupling_ref, out_ref):
    @pl.when(pl.program_id(0) == 0)
    def _():
        out_ref[...] = jnp.zeros_like(out_ref)

    out_ref[...] += jnp.dot(
        left_ref[...], coupling_ref[...], preferred_element_type=F32
    )


def shadow_kernel(left_ref, coupling_ref, out_ref):
    out_ref[...] = lax.dot_general(
        left_ref[...],
        coupling_ref[...],
        (((1,), (1,)), ((), ())),
        preferred_element_type=F32,
    )


def call(kernel, name, left, coupling, left_spec, out_spec, width):
    rows, columns = coupling.shape
    reps = left.shape[0]
    return pl.pallas_call(
        kernel,
        name=name,
        grid=(rows // TILE,),
        in_specs=[left_spec, pl.BlockSpec((TILE, columns), lambda i: (i, 0))],
        out_specs=out_spec,
        out_shape=jax.ShapeDtypeStruct((reps, width), F32),
        compiler_params=pltpu.CompilerParams(vmem_limit_bytes=52 << 20),
        cost_estimate=pl.CostEstimate(
            flops=2 * reps * rows * columns,
            bytes_accessed=2 * rows * columns,
            transcendentals=0,
        ),
    )(left, coupling)


def primary(left, coupling):
    reps, columns = left.shape[0], coupling.shape[1]
    return call(
        primary_kernel,
        "primary",
        left,
        coupling,
        pl.BlockSpec((reps, TILE), lambda i: (0, i)),
        pl.BlockSpec((reps, columns), lambda i: (0, 0)),
        columns,
    )


def shadow(left, coupling):
    reps, columns = left.shape
    return call(
        shadow_kernel,
        "shadow",
        left,
        coupling,
        pl.BlockSpec((reps, columns), lambda i: (0, 0)),
        pl.BlockSpec((reps, TILE), lambda i: (0, i)),
        coupling.shape[0],
    )


def move(value, pairs):
    return lax.ppermute(value, AXES, pairs)


def chip_sum(value, steps):
    for pairs in steps:
        held = value.astype(WIRE)
        value = held.astype(F32) + move(held, pairs).astype(F32)
    return value


def pick(flag, value):
    width = value.shape[1] // 2
    low, high = value[:, :width], value[:, width:]
    return jnp.where(flag, low, high), jnp.where(flag, high, low)


def put(flag, mine, other):
    low = jnp.where(flag, mine, other)
    high = jnp.where(flag, other, mine)
    return jnp.concatenate([low, high], axis=1)


SENDS_LOW = [0] * 128
for source, destination in TO_ROWS:
    SENDS_LOW[source] = int(split(destination)[3] % 2 == 0)


def z_even_source(row, col):
    return jnp.array(SENDS_LOW, jnp.int32)[row * 16 + col] == 1


def total(value):
    return jnp.sum(value, axis=1)


def on_device(coupling, amplitude, target, shadow_target):
    row, col = lax.axis_index("row"), lax.axis_index("col")
    x, yh = row >> 1, row & 1
    first = (col & 1) == 0
    z_even = (col & 2) == 0
    low_half = jnp.where(first, (x ^ (x >> 1)) & 1, yh) == 0

    g, gs = target, shadow_target
    slope = 1.0 - amplitude * amplitude
    keep = 1.0 - SELF_GAIN * slope

    def spread(half):
        mine = put(z_even, half, move(half, Z_PAIR))
        return mine, put(first, mine, move(mine, CORE))

    half = pick(z_even_source(row, col), (slope * g).astype(BF16))[0]
    half = move(half, TO_ROWS)
    shadow_partial = shadow(gs.astype(BF16), coupling)
    half, shadow_partial = lax.optimization_barrier((half, shadow_partial))

    tops = jnp.stack([jnp.max(jnp.abs(g), axis=1), jnp.max(jnp.abs(gs), axis=1)])
    stats = jnp.concatenate([tops, jnp.stack([total(gs * g), total(gs * (keep * g))])])
    for pairs in SMALL_COL:
        other = move(stats, pairs)
        stats = jnp.concatenate(
            [jnp.maximum(stats[:2], other[:2]), stats[2:] + other[2:]]
        )
    tiny = 1e-30
    top = jnp.maximum(stats[0], tiny)[:, None]
    shadow_top = jnp.maximum(stats[1], tiny)[:, None]
    align = stats[2]
    alpha = jnp.clip(stats[2] / stats[3], 1.0, 2.05)
    alpha = jnp.where(jnp.isnan(alpha), 1.4, alpha)
    alpha_c = alpha[:, None]

    def shadow_sum(partial, scale):
        mine, other = pick(first, partial)
        mine = mine * scale + move((other * scale).astype(WIRE), CORE).astype(F32)
        rows = chip_sum(mine, COL_STEPS).astype(WIRE)
        return rows, move(rows, TO_COLS)

    _, left = spread(half)
    primary_partial = primary(left, coupling)
    scale = FIRST_SCALE / top
    mine, other = pick(low_half, primary_partial * scale)
    mine = mine + move(other.astype(WIRE), ROW_STEPS[0]).astype(F32)
    mine = chip_sum(mine, ROW_STEPS[1:]).astype(WIRE)
    unscale = COUPLE_GAIN / scale

    def first_step(kept, value, product):
        image = kept * value - product.astype(F32) * unscale
        return image, value - alpha_c * image

    g_half, keep_half = pick(low_half, g)[0], pick(low_half, keep)[0]
    slope_half = pick(low_half, slope)[0]
    _, u_half = first_step(keep_half, g_half, mine)
    u_half = (slope_half * u_half).astype(BF16)
    u_half = move(u_half, HALF_TO_ROWS)
    product = put(low_half, mine, move(mine, ROW_STEPS[0]))
    p1, u = first_step(keep, g, product)

    scale = FIRST_SCALE / shadow_top
    _, columns = shadow_sum(shadow_partial, scale)
    q1 = keep * gs - (COUPLE_GAIN / scale) * slope * columns.astype(F32)
    us = gs - alpha_c * q1

    shadow_partial = shadow(us.astype(BF16), coupling)
    u_rows, left = spread(u_half)
    primary_partial = primary(left, coupling)
    scale = SECOND_SCALE / shadow_top
    rows, columns = shadow_sum(shadow_partial, scale)
    last = total(u_rows.astype(F32) * rows.astype(F32)) / scale[:, 0]
    q2 = keep * us - (COUPLE_GAIN / scale) * slope * columns.astype(F32)
    scale = SECOND_SCALE / top
    product = chip_sum(primary_partial * scale, ROW_STEPS)
    p2 = keep * u - (COUPLE_GAIN / scale) * product

    for pairs in SMALL_ROW:
        last = last + move(last, pairs)
    dots = jnp.stack(
        [
            total(gs * p1),
            total(us * g),
            total(us * u),
            total(us * p1),
            total(q1 * u),
            total(us * (keep * u)),
        ]
    )
    for pairs in SMALL_COL:
        dots = dots + move(dots, pairs)
    curve, us_g, us_u, us_p1, q1_u, us_kept = (dots[i] for i in range(6))
    us_p2 = us_kept - COUPLE_GAIN * last
    gs_u = align - alpha * curve
    step = align / curve
    kappa = step / alpha
    rest = 1.0 - kappa
    align_next = (
        rest * rest * align + kappa * rest * (us_g + gs_u) + kappa * kappa * us_u
    )
    blend = align_next / align
    lead = rest + blend
    curve_next = (
        lead * lead * curve + lead * kappa * (us_p1 + q1_u) + kappa * kappa * us_p2
    )
    step_next = align_next / curve_next

    def column(value):
        return value[:, None]

    step, kappa, lead, step_next = map(column, (step, kappa, lead, step_next))
    direction = lead * g + kappa * u
    shadow_direction = lead * gs + kappa * us
    solution = step * g + step_next * direction
    shadow_solution = step * gs + step_next * shadow_direction
    residual = g - step * p1 - step_next * (lead * p1 + kappa * p2)
    shadow_residual = gs - step * q1 - step_next * (lead * q1 + kappa * q2)
    return (solution, shadow_solution, residual, shadow_residual)


def solution(mesh):
    return jax.shard_map(
        on_device,
        mesh=mesh,
        in_specs=(P("row", "col"), P(None, "col"), P(None, "col"), P(None, "col")),
        out_specs=(P(None, "col"), P(None, "col"), P(None, "col"), P(None, "col")),
        check_vma=False,
    )
```

```python
import jax
import jax.numpy as jnp
from jax import lax
from jax.experimental import pallas as pl
from jax.experimental.pallas import tpu as pltpu
from jax.sharding import PartitionSpec as P

SELF_GAIN = 0.5
COUPLE_GAIN = 0.3

F32 = jnp.float32
BF16 = jnp.bfloat16
WIRE = jnp.float16
AXES = ("row", "col")

FIRST_SCALE = 32.0
SECOND_SCALE = 1.0 / 16.0


def split(d):
    row, col = divmod(d, 16)
    return row // 2, row % 2, col // 8, (col // 2) % 4, col % 2


def join(x, yh, yl, z, h):
    return (x * 2 + yh) * 16 + yl * 8 + z * 2 + h


def sends(source_of):
    return [(join(*source_of(*split(d))), d) for d in range(128)]


def flip_x(x, yh, yl, z, h):
    return x ^ 1, yh, yl, z, h


def mirror_x(x, yh, yl, z, h):
    return 3 - x, yh, yl, z, h


def flip_yh(x, yh, yl, z, h):
    return x, yh ^ 1, yl, z, h


def flip_yl(x, yh, yl, z, h):
    return x, yh, yl ^ 1, z, h


def flip_z(x, yh, yl, z, h):
    return x, yh, yl, z ^ 1, h


def mirror_z(x, yh, yl, z, h):
    return x, yh, yl, 3 - z, h


def flip_core(x, yh, yl, z, h):
    return x, yh, yl, z, h ^ 1


def by_core(first, second):
    return sends(lambda *d: (second if d[4] else first)(*d))


STEP = ({0: 2, 1: 1, 2: 0, 3: 3}, {0: 2, 1: 3, 2: 0, 3: 1})


def from_rows(x, yh, yl, z, h):
    xs, yhs = 2 * yl + z // 2, z % 2
    return xs, yhs, yl ^ yh ^ yhs, (z + STEP[h][(x - xs) % 4]) % 4, h


HALF_SOURCE = (
    7, 4, 3, 7, 0, 2, 4, 1, 6, 6, 2, 3, 1, 0, 5, 5,
    7, 0, 2, 5, 0, 6, 5, 7, 6, 2, 4, 3, 1, 4, 3, 1,
    6, 0, 4, 1, 1, 6, 3, 3, 0, 2, 2, 7, 7, 4, 5, 5,
    0, 4, 5, 1, 7, 2, 2, 7, 1, 0, 3, 3, 6, 6, 4, 5,
    0, 6, 3, 7, 7, 4, 4, 1, 1, 0, 5, 3, 6, 2, 2, 5,
    7, 2, 3, 7, 0, 0, 4, 5, 1, 6, 2, 1, 6, 4, 5, 3,
    6, 6, 4, 3, 1, 0, 3, 5, 0, 4, 5, 7, 7, 2, 2, 1,
    0, 4, 5, 7, 7, 2, 2, 1, 6, 0, 3, 5, 1, 6, 4, 3,
)

CORE = sends(flip_core)
TO_COLS = sends(from_rows)
HALF_TO_ROWS = [
    (HALF_SOURCE[d] * 16 + (d // 16) * 2 + d % 2, d) for d in range(128)
]
ROW_STEPS = (
    by_core(flip_x, flip_yh),
    by_core(mirror_x, flip_x),
    by_core(flip_yh, mirror_x),
)
COL_STEPS = (
    by_core(flip_yl, flip_z),
    by_core(flip_z, mirror_z),
    by_core(mirror_z, flip_yl),
)
Z_PAIR = sends(flip_z)
SMALL_COL = (CORE, sends(flip_yl), sends(flip_z), sends(mirror_z))

def fetch(source_ref, held_ref, sems):
    chunks = sems.shape[0]
    size = source_ref.shape[0] // chunks
    copies = []
    for i in range(chunks):
        at = pl.ds(i * size, size)
        copies.append(
            pltpu.make_async_copy(source_ref.at[at], held_ref.at[at], sems.at[i])
        )
        copies[-1].start()
    for i, copy in enumerate(copies):
        copy.wait()
        yield i, pl.ds(i * size, size)


def primary_kernel(left_ref, coupling_ref, out_ref, held_ref, sems):
    for i, at in fetch(coupling_ref, held_ref, sems):
        term = jnp.dot(left_ref[:, at], held_ref[at, :], preferred_element_type=F32)
        if i == 0:
            out_ref[...] = term
        else:
            out_ref[...] += term


def shadow_kernel(left_ref, coupling_ref, out_ref, held_ref, sems):
    for _, at in fetch(coupling_ref, held_ref, sems):
        out_ref[:, at] = lax.dot_general(
            left_ref[...],
            held_ref[at, :],
            (((1,), (1,)), ((), ())),
            preferred_element_type=F32,
        )


def call(kernel, name, left, coupling, width, chunks):
    rows, columns = coupling.shape
    reps = left.shape[0]
    spec = pl.BlockSpec(memory_space=pltpu.VMEM)
    return pl.pallas_call(
        kernel,
        name=name,
        in_specs=[spec, pl.BlockSpec(memory_space=pltpu.HBM)],
        out_specs=spec,
        out_shape=jax.ShapeDtypeStruct((reps, width), F32),
        scratch_shapes=[
            pltpu.VMEM((rows, columns), BF16),
            pltpu.SemaphoreType.DMA((chunks,)),
        ],
        compiler_params=pltpu.CompilerParams(vmem_limit_bytes=24 << 20),
        cost_estimate=pl.CostEstimate(
            flops=2 * reps * rows * columns,
            bytes_accessed=2 * rows * columns,
            transcendentals=0,
        ),
    )(left, coupling)


def primary(left, coupling):
    return call(primary_kernel, "primary", left, coupling, coupling.shape[1], 16)


def shadow(left, coupling):
    return call(shadow_kernel, "shadow", left, coupling, coupling.shape[0], 8)


def move(value, pairs):
    return lax.ppermute(value, AXES, pairs)


def chip_sum(value, steps):
    for pairs in steps:
        held = value.astype(WIRE)
        value = held.astype(F32) + move(held, pairs).astype(F32)
    return value


def pick(flag, value):
    width = value.shape[1] // 2
    low, high = value[:, :width], value[:, width:]
    return jnp.where(flag, low, high), jnp.where(flag, high, low)


def put(flag, mine, other):
    low = jnp.where(flag, mine, other)
    high = jnp.where(flag, other, mine)
    return jnp.concatenate([low, high], axis=1)


def total(value):
    return jnp.sum(value, axis=1)


def on_device(coupling, amplitude, target, shadow_target):
    row, col = lax.axis_index("row"), lax.axis_index("col")
    x, yh = row >> 1, row & 1
    first = (col & 1) == 0
    z_even = (col & 2) == 0
    low_half = jnp.where(first, (x ^ (x >> 1)) & 1, yh) == 0

    coupling = pltpu.with_memory_space_constraint(coupling, pltpu.HBM)
    g, gs = target, shadow_target
    slope = 1.0 - amplitude * amplitude
    keep = 1.0 - SELF_GAIN * slope

    def spread(half):
        mine = put(z_even, half, move(half, Z_PAIR))
        return put(first, mine, move(mine, CORE))

    half = pick(low_half, (slope * g).astype(BF16))[0]
    half = move(half, HALF_TO_ROWS)
    shadow_partial = shadow(gs.astype(BF16), coupling)

    tops = jnp.stack([jnp.max(jnp.abs(g), axis=1), jnp.max(jnp.abs(gs), axis=1)])
    stats = jnp.concatenate([tops, jnp.stack([total(gs * g), total(gs * (keep * g))])])
    for pairs in SMALL_COL:
        if pairs is SMALL_COL[2]:
            stats, half, shadow_partial = lax.optimization_barrier(
                (stats, half, shadow_partial)
            )
        other = move(stats, pairs)
        stats = jnp.concatenate(
            [jnp.maximum(stats[:2], other[:2]), stats[2:] + other[2:]]
        )
    tiny = 1e-30
    top = jnp.maximum(stats[0], tiny)[:, None]
    shadow_top = jnp.maximum(stats[1], tiny)[:, None]
    align = stats[2]
    alpha = jnp.clip(stats[2] / stats[3], 1.0, 2.05)
    alpha = jnp.where(jnp.isnan(alpha), 1.4, alpha)
    alpha_c = alpha[:, None]

    def core_sum(partial, scale):
        mine, other = pick(first, partial)
        return mine * scale + move((other * scale).astype(WIRE), CORE).astype(F32)

    left = spread(half)
    primary_partial = primary(left, coupling)
    scale = FIRST_SCALE / top
    mine, other = pick(low_half, primary_partial * scale)
    mine = mine + move(other.astype(WIRE), ROW_STEPS[0]).astype(F32)
    mine = chip_sum(mine, ROW_STEPS[1:]).astype(WIRE)
    unscale = COUPLE_GAIN / scale

    def first_step(kept, value, product):
        image = kept * value - product.astype(F32) * unscale
        return image, value - alpha_c * image

    g_half, keep_half = pick(low_half, g)[0], pick(low_half, keep)[0]
    slope_half = pick(low_half, slope)[0]
    _, u_half = first_step(keep_half, g_half, mine)
    u_half = (slope_half * u_half).astype(BF16)
    u_half = move(u_half, HALF_TO_ROWS)
    scale = FIRST_SCALE / shadow_top
    columns = chip_sum(core_sum(shadow_partial, scale), COL_STEPS)
    columns = move(columns.astype(WIRE), TO_COLS)
    q1 = keep * gs - (COUPLE_GAIN / scale) * slope * columns.astype(F32)
    us = gs - alpha_c * q1

    left = spread(u_half)
    primary_partial = primary(left, coupling)
    us_sent, mine, primary_partial = lax.optimization_barrier(
        (us.astype(BF16), mine, primary_partial)
    )
    shadow_partial = shadow(us_sent, coupling)
    scale = SECOND_SCALE / top
    second = chip_sum(primary_partial * scale, ROW_STEPS) * (COUPLE_GAIN / scale)
    product = put(low_half, mine, move(mine, ROW_STEPS[0]))
    p1, u = first_step(keep, g, product)
    p2 = keep * u - second

    dots = jnp.stack(
        [
            total(gs * p1),
            total(us * g),
            total(us * u),
            total(us * p1),
            total(q1 * u),
            total(us * p2),
        ]
    )
    for pairs in SMALL_COL[:2]:
        dots = dots + move(dots, pairs)
    scale = SECOND_SCALE / shadow_top
    held = chip_sum(core_sum(shadow_partial, scale), COL_STEPS[:2]).astype(WIRE)
    held, dots = lax.optimization_barrier((held, dots))
    columns = move(chip_sum(held, COL_STEPS[2:]).astype(WIRE), TO_COLS)
    for pairs in SMALL_COL[2:]:
        dots = dots + move(dots, pairs)
    curve, us_g, us_u, us_p1, q1_u, us_p2 = (dots[i] for i in range(6))
    q2 = keep * us - (COUPLE_GAIN / scale) * slope * columns.astype(F32)

    gs_u = align - alpha * curve
    step = align / curve
    kappa = step / alpha
    rest = 1.0 - kappa
    align_next = (
        rest * rest * align + kappa * rest * (us_g + gs_u) + kappa * kappa * us_u
    )
    blend = align_next / align
    lead = rest + blend
    curve_next = (
        lead * lead * curve + lead * kappa * (us_p1 + q1_u) + kappa * kappa * us_p2
    )
    step_next = align_next / curve_next

    def column(value):
        return value[:, None]

    step, kappa, lead, step_next = map(column, (step, kappa, lead, step_next))
    direction = lead * g + kappa * u
    shadow_direction = lead * gs + kappa * us
    solution = step * g + step_next * direction
    shadow_solution = step * gs + step_next * shadow_direction
    residual = g - step * p1 - step_next * (lead * p1 + kappa * p2)
    shadow_residual = gs - step * q1 - step_next * (lead * q1 + kappa * q2)
    return (solution, shadow_solution, residual, shadow_residual)


def solution(mesh):
    return jax.shard_map(
        on_device,
        mesh=mesh,
        in_specs=(P("row", "col"), P(None, "col"), P(None, "col"), P(None, "col")),
        out_specs=(P(None, "col"), P(None, "col"), P(None, "col"), P(None, "col")),
        check_vma=False,
    )
```

```python
import jax
import jax.numpy as jnp
from jax import lax
from jax.experimental import pallas as pl
from jax.experimental.pallas import tpu as pltpu
from jax.sharding import PartitionSpec as P

SELF_GAIN = 0.5
COUPLE_GAIN = 0.3

F32 = jnp.float32
BF16 = jnp.bfloat16
WIRE = jnp.float16
AXES = ("row", "col")

FIRST_SCALE = 32.0
SECOND_SCALE = 1.0 / 16.0


def split(d):
    row, col = divmod(d, 16)
    return row // 2, row % 2, col // 8, (col // 2) % 4, col % 2


def join(x, yh, yl, z, h):
    return (x * 2 + yh) * 16 + yl * 8 + z * 2 + h


def sends(source_of):
    return [(join(*source_of(*split(d))), d) for d in range(128)]


def flip_x(x, yh, yl, z, h):
    return x ^ 1, yh, yl, z, h


def mirror_x(x, yh, yl, z, h):
    return 3 - x, yh, yl, z, h


def flip_yh(x, yh, yl, z, h):
    return x, yh ^ 1, yl, z, h


def flip_yl(x, yh, yl, z, h):
    return x, yh, yl ^ 1, z, h


def flip_z(x, yh, yl, z, h):
    return x, yh, yl, z ^ 1, h


def mirror_z(x, yh, yl, z, h):
    return x, yh, yl, 3 - z, h


def flip_core(x, yh, yl, z, h):
    return x, yh, yl, z, h ^ 1


def by_core(first, second):
    return sends(lambda *d: (second if d[4] else first)(*d))


STEP = ({0: 2, 1: 1, 2: 0, 3: 3}, {0: 2, 1: 3, 2: 0, 3: 1})


def from_rows(x, yh, yl, z, h):
    xs, yhs = 2 * yl + z // 2, z % 2
    return xs, yhs, yl ^ yh ^ yhs, (z + STEP[h][(x - xs) % 4]) % 4, h


HALF_SOURCE = (
    7, 4, 3, 7, 0, 2, 4, 1, 6, 6, 2, 3, 1, 0, 5, 5,
    7, 0, 2, 5, 0, 6, 5, 7, 6, 2, 4, 3, 1, 4, 3, 1,
    6, 0, 4, 1, 1, 6, 3, 3, 0, 2, 2, 7, 7, 4, 5, 5,
    0, 4, 5, 1, 7, 2, 2, 7, 1, 0, 3, 3, 6, 6, 4, 5,
    0, 6, 3, 7, 7, 4, 4, 1, 1, 0, 5, 3, 6, 2, 2, 5,
    7, 2, 3, 7, 0, 0, 4, 5, 1, 6, 2, 1, 6, 4, 5, 3,
    6, 6, 4, 3, 1, 0, 3, 5, 0, 4, 5, 7, 7, 2, 2, 1,
    0, 4, 5, 7, 7, 2, 2, 1, 6, 0, 3, 5, 1, 6, 4, 3,
)

CORE = sends(flip_core)
TO_COLS = sends(from_rows)
HALF_TO_ROWS = [
    (HALF_SOURCE[d] * 16 + (d // 16) * 2 + d % 2, d) for d in range(128)
]
ROW_STEPS = (
    by_core(flip_x, flip_yh),
    by_core(mirror_x, flip_x),
    by_core(flip_yh, mirror_x),
)
COL_STEPS = (
    by_core(flip_yl, flip_z),
    by_core(flip_z, mirror_z),
    by_core(mirror_z, flip_yl),
)
Z_PAIR = sends(flip_z)
SMALL_COL = (CORE, sends(flip_yl), sends(flip_z), sends(mirror_z))

def fetch(source_ref, held_ref, sems):
    chunks = sems.shape[0]
    size = source_ref.shape[0] // chunks
    copies = []
    for i in range(chunks):
        at = pl.ds(i * size, size)
        copies.append(
            pltpu.make_async_copy(source_ref.at[at], held_ref.at[at], sems.at[i])
        )
        copies[-1].start()
    for i, copy in enumerate(copies):
        copy.wait()
        yield i, pl.ds(i * size, size)


def primary_kernel(left_ref, coupling_ref, out_ref, held_ref, sems):
    for i, at in fetch(coupling_ref, held_ref, sems):
        term = jnp.dot(left_ref[:, at], held_ref[at, :], preferred_element_type=F32)
        if i == 0:
            out_ref[...] = term
        else:
            out_ref[...] += term


def shadow_kernel(left_ref, coupling_ref, out_ref, held_ref, sems):
    for _, at in fetch(coupling_ref, held_ref, sems):
        out_ref[:, at] = lax.dot_general(
            left_ref[...],
            held_ref[at, :],
            (((1,), (1,)), ((), ())),
            preferred_element_type=F32,
        )


def call(kernel, name, left, coupling, width, chunks):
    rows, columns = coupling.shape
    reps = left.shape[0]
    spec = pl.BlockSpec(memory_space=pltpu.VMEM)
    return pl.pallas_call(
        kernel,
        name=name,
        in_specs=[spec, pl.BlockSpec(memory_space=pltpu.HBM)],
        out_specs=spec,
        out_shape=jax.ShapeDtypeStruct((reps, width), F32),
        scratch_shapes=[
            pltpu.VMEM((rows, columns), BF16),
            pltpu.SemaphoreType.DMA((chunks,)),
        ],
        compiler_params=pltpu.CompilerParams(vmem_limit_bytes=24 << 20),
        cost_estimate=pl.CostEstimate(
            flops=2 * reps * rows * columns,
            bytes_accessed=2 * rows * columns,
            transcendentals=0,
        ),
    )(left, coupling)


def primary(left, coupling):
    return call(primary_kernel, "primary", left, coupling, coupling.shape[1], 16)


def shadow(left, coupling):
    return call(shadow_kernel, "shadow", left, coupling, coupling.shape[0], 8)


def move(value, pairs):
    return lax.ppermute(value, AXES, pairs)


def exchange(held, pairs):
    return (held.astype(F32) + move(held, pairs).astype(F32)).astype(WIRE)


def tie(*values):
    return lax.optimization_barrier(values)


def pick(flag, value):
    width = value.shape[1] // 2
    low, high = value[:, :width], value[:, width:]
    return jnp.where(flag, low, high), jnp.where(flag, high, low)


def put(flag, mine, other):
    low = jnp.where(flag, mine, other)
    high = jnp.where(flag, other, mine)
    return jnp.concatenate([low, high], axis=1)


def total(value):
    return jnp.sum(value, axis=1)


def on_device(coupling, amplitude, target, shadow_target):
    row, col = lax.axis_index("row"), lax.axis_index("col")
    x, yh = row >> 1, row & 1
    first = (col & 1) == 0
    z_even = (col & 2) == 0
    low_half = jnp.where(first, (x ^ (x >> 1)) & 1, yh) == 0

    coupling = pltpu.with_memory_space_constraint(coupling, pltpu.HBM)
    g, gs = target, shadow_target
    slope = 1.0 - amplitude * amplitude
    keep = 1.0 - SELF_GAIN * slope

    def send_core(partial, scale):
        mine, other = pick(first, partial * scale)
        return (mine + move(other.astype(WIRE), CORE).astype(F32)).astype(WIRE)

    def send_half(mine, other):
        return (mine + move(other.astype(WIRE), ROW_STEPS[0]).astype(F32)).astype(WIRE)

    half = pick(low_half, (slope * g).astype(BF16))[0]
    half = move(half, HALF_TO_ROWS)
    shadow_partial = shadow(gs.astype(BF16), coupling)

    tops = jnp.stack([jnp.max(jnp.abs(g), axis=1), jnp.max(jnp.abs(gs), axis=1)])
    stats = jnp.concatenate([tops, jnp.stack([total(gs * g), total(gs * (keep * g))])])
    for pairs in SMALL_COL:
        if pairs is SMALL_COL[2]:
            stats, half, shadow_partial = tie(stats, half, shadow_partial)
        other = move(stats, pairs)
        stats = jnp.concatenate(
            [jnp.maximum(stats[:2], other[:2]), stats[2:] + other[2:]]
        )
    tiny = 1e-30
    top = jnp.maximum(stats[0], tiny)[:, None]
    shadow_top = jnp.maximum(stats[1], tiny)[:, None]
    align = stats[2]
    alpha = jnp.clip(stats[2] / stats[3], 1.0, 2.05)
    alpha = jnp.where(jnp.isnan(alpha), 1.4, alpha)
    alpha_c = alpha[:, None]

    block = put(z_even, half, move(half, Z_PAIR))
    left = put(first, block, move(block, CORE))
    shadow_held = send_core(shadow_partial, FIRST_SCALE / shadow_top)
    left, shadow_held = tie(left, shadow_held)
    partial = primary(left, coupling)
    shadow_held = exchange(shadow_held, COL_STEPS[0])
    partial, shadow_held = tie(partial, shadow_held)
    scale = FIRST_SCALE / top
    held = send_half(*pick(low_half, partial * scale))
    shadow_held = exchange(shadow_held, COL_STEPS[1])
    held, shadow_held = tie(held, shadow_held)
    held = exchange(held, ROW_STEPS[1])
    shadow_held = exchange(shadow_held, COL_STEPS[2])
    held, shadow_held = tie(held, shadow_held)
    columns = move(shadow_held, TO_COLS)
    held = exchange(held, ROW_STEPS[2])
    held, columns = tie(held, columns)

    unscale = COUPLE_GAIN / scale

    def first_step(kept, value, product):
        image = kept * value - product.astype(F32) * unscale
        return image, value - alpha_c * image

    g_half, keep_half = pick(low_half, g)[0], pick(low_half, keep)[0]
    slope_half = pick(low_half, slope)[0]
    _, u_half = first_step(keep_half, g_half, held)
    half = move((slope_half * u_half).astype(BF16), HALF_TO_ROWS)
    scale = FIRST_SCALE / shadow_top
    q1 = keep * gs - (COUPLE_GAIN / scale) * slope * columns.astype(F32)
    us = gs - alpha_c * q1

    shadow_partial = shadow(us.astype(BF16), coupling)
    half, shadow_partial, held = tie(half, shadow_partial, held)
    block = put(z_even, half, move(half, Z_PAIR))
    scale = SECOND_SCALE / shadow_top
    shadow_held = send_core(shadow_partial, scale)
    product = put(low_half, held, move(held, ROW_STEPS[0]))
    block, shadow_held, product = tie(block, shadow_held, product)
    left = put(first, block, move(block, CORE))
    partial = primary(left, coupling)
    shadow_held = exchange(shadow_held, COL_STEPS[0])
    partial, shadow_held = tie(partial, shadow_held)
    held = exchange((partial * (SECOND_SCALE / top)).astype(WIRE), ROW_STEPS[0])
    shadow_held = exchange(shadow_held, COL_STEPS[1])
    held, shadow_held = tie(held, shadow_held)
    held = exchange(held, ROW_STEPS[1])
    shadow_held = exchange(shadow_held, COL_STEPS[2])
    held, shadow_held = tie(held, shadow_held)
    columns = move(shadow_held, TO_COLS)
    held = exchange(held, ROW_STEPS[2])

    p1, u = first_step(keep, g, product)
    p2 = keep * u - held.astype(F32) * (COUPLE_GAIN * top / SECOND_SCALE)
    dots = jnp.stack(
        [
            total(gs * p1),
            total(us * g),
            total(us * u),
            total(us * p1),
            total(q1 * u),
            total(us * p2),
        ]
    )
    for pairs in SMALL_COL:
        if pairs is SMALL_COL[1]:
            dots, columns = tie(dots, columns)
        dots = dots + move(dots, pairs)
    curve, us_g, us_u, us_p1, q1_u, us_p2 = (dots[i] for i in range(6))
    q2 = keep * us - (COUPLE_GAIN / scale) * slope * columns.astype(F32)

    gs_u = align - alpha * curve
    step = align / curve
    kappa = step / alpha
    rest = 1.0 - kappa
    align_next = (
        rest * rest * align + kappa * rest * (us_g + gs_u) + kappa * kappa * us_u
    )
    blend = align_next / align
    lead = rest + blend
    curve_next = (
        lead * lead * curve + lead * kappa * (us_p1 + q1_u) + kappa * kappa * us_p2
    )
    step_next = align_next / curve_next

    def column(value):
        return value[:, None]

    step, kappa, lead, step_next = map(column, (step, kappa, lead, step_next))
    direction = lead * g + kappa * u
    shadow_direction = lead * gs + kappa * us
    solution = step * g + step_next * direction
    shadow_solution = step * gs + step_next * shadow_direction
    residual = g - step * p1 - step_next * (lead * p1 + kappa * p2)
    shadow_residual = gs - step * q1 - step_next * (lead * q1 + kappa * q2)
    return (solution, shadow_solution, residual, shadow_residual)


def solution(mesh):
    return jax.shard_map(
        on_device,
        mesh=mesh,
        in_specs=(P("row", "col"), P(None, "col"), P(None, "col"), P(None, "col")),
        out_specs=(P(None, "col"), P(None, "col"), P(None, "col"), P(None, "col")),
        check_vma=False,
    )
```

```python
import jax
import jax.numpy as jnp
from jax import lax
from jax.experimental import pallas as pl
from jax.experimental.pallas import tpu as pltpu
from jax.sharding import PartitionSpec as P

SELF_GAIN = 0.5
COUPLE_GAIN = 0.3

F32 = jnp.float32
BF16 = jnp.bfloat16
WIRE = jnp.float16
AXES = ("row", "col")

FIRST_SCALE = 32.0
SECOND_SCALE = 1.0 / 16.0


def split(d):
    row, col = divmod(d, 16)
    return row // 2, row % 2, col // 8, (col // 2) % 4, col % 2


def join(x, yh, yl, z, h):
    return (x * 2 + yh) * 16 + yl * 8 + z * 2 + h


def sends(source_of):
    return [(join(*source_of(*split(d))), d) for d in range(128)]


def flip_x(x, yh, yl, z, h):
    return x ^ 1, yh, yl, z, h


def mirror_x(x, yh, yl, z, h):
    return 3 - x, yh, yl, z, h


def flip_yh(x, yh, yl, z, h):
    return x, yh ^ 1, yl, z, h


def flip_yl(x, yh, yl, z, h):
    return x, yh, yl ^ 1, z, h


def flip_z(x, yh, yl, z, h):
    return x, yh, yl, z ^ 1, h


def mirror_z(x, yh, yl, z, h):
    return x, yh, yl, 3 - z, h


def flip_core(x, yh, yl, z, h):
    return x, yh, yl, z, h ^ 1


def by_core(first, second):
    return sends(lambda *d: (second if d[4] else first)(*d))


STEP = ({0: 2, 1: 1, 2: 0, 3: 3}, {0: 2, 1: 3, 2: 0, 3: 1})


def from_rows(x, yh, yl, z, h):
    xs, yhs = 2 * yl + z // 2, z % 2
    return xs, yhs, yl ^ yh ^ yhs, (z + STEP[h][(x - xs) % 4]) % 4, h


HALF_SOURCE = (
    7, 4, 3, 7, 0, 2, 4, 1, 6, 6, 2, 3, 1, 0, 5, 5,
    7, 0, 2, 5, 0, 6, 5, 7, 6, 2, 4, 3, 1, 4, 3, 1,
    6, 0, 4, 1, 1, 6, 3, 3, 0, 2, 2, 7, 7, 4, 5, 5,
    0, 4, 5, 1, 7, 2, 2, 7, 1, 0, 3, 3, 6, 6, 4, 5,
    0, 6, 3, 7, 7, 4, 4, 1, 1, 0, 5, 3, 6, 2, 2, 5,
    7, 2, 3, 7, 0, 0, 4, 5, 1, 6, 2, 1, 6, 4, 5, 3,
    6, 6, 4, 3, 1, 0, 3, 5, 0, 4, 5, 7, 7, 2, 2, 1,
    0, 4, 5, 7, 7, 2, 2, 1, 6, 0, 3, 5, 1, 6, 4, 3,
)

CORE = sends(flip_core)
TO_COLS = sends(from_rows)
HALF_TO_ROWS = [
    (HALF_SOURCE[d] * 16 + (d // 16) * 2 + d % 2, d) for d in range(128)
]
ROW_STEPS = (
    by_core(flip_x, flip_yh),
    by_core(mirror_x, flip_x),
    by_core(flip_yh, mirror_x),
)
COL_STEPS = (
    by_core(flip_yl, flip_z),
    by_core(flip_z, mirror_z),
    by_core(mirror_z, flip_yl),
)
Z_PAIR = sends(flip_z)
SMALL_ROW = (CORE, sends(flip_x), sends(mirror_x), sends(flip_yh))
SMALL_COL = (CORE, sends(flip_yl), sends(flip_z), sends(mirror_z))

def fetch(source_ref, held_ref, sems):
    chunks = sems.shape[0]
    size = source_ref.shape[0] // chunks
    copies = []
    for i in range(chunks):
        at = pl.ds(i * size, size)
        copies.append(
            pltpu.make_async_copy(source_ref.at[at], held_ref.at[at], sems.at[i])
        )
        copies[-1].start()
    for i, copy in enumerate(copies):
        copy.wait()
        yield i, pl.ds(i * size, size)


def primary_kernel(left_ref, coupling_ref, out_ref, held_ref, sems):
    for i, at in fetch(coupling_ref, held_ref, sems):
        term = jnp.dot(left_ref[:, at], held_ref[at, :], preferred_element_type=F32)
        if i == 0:
            out_ref[...] = term
        else:
            out_ref[...] += term


def shadow_kernel(left_ref, coupling_ref, out_ref, held_ref, sems):
    for _, at in fetch(coupling_ref, held_ref, sems):
        out_ref[:, at] = lax.dot_general(
            left_ref[...],
            held_ref[at, :],
            (((1,), (1,)), ((), ())),
            preferred_element_type=F32,
        )


def call(kernel, name, left, coupling, width, chunks):
    rows, columns = coupling.shape
    reps = left.shape[0]
    spec = pl.BlockSpec(memory_space=pltpu.VMEM)
    return pl.pallas_call(
        kernel,
        name=name,
        in_specs=[spec, pl.BlockSpec(memory_space=pltpu.HBM)],
        out_specs=spec,
        out_shape=jax.ShapeDtypeStruct((reps, width), F32),
        scratch_shapes=[
            pltpu.VMEM((rows, columns), BF16),
            pltpu.SemaphoreType.DMA((chunks,)),
        ],
        compiler_params=pltpu.CompilerParams(vmem_limit_bytes=24 << 20),
        cost_estimate=pl.CostEstimate(
            flops=2 * reps * rows * columns,
            bytes_accessed=2 * rows * columns,
            transcendentals=0,
        ),
    )(left, coupling)


def primary(left, coupling):
    return call(primary_kernel, "primary", left, coupling, coupling.shape[1], 16)


def shadow(left, coupling):
    return call(shadow_kernel, "shadow", left, coupling, coupling.shape[0], 8)


def move(value, pairs):
    return lax.ppermute(value, AXES, pairs)


def exchange(held, pairs):
    return (held.astype(F32) + move(held, pairs).astype(F32)).astype(WIRE)


def tie(*values):
    return lax.optimization_barrier(values)


def pick(flag, value):
    width = value.shape[1] // 2
    low, high = value[:, :width], value[:, width:]
    return jnp.where(flag, low, high), jnp.where(flag, high, low)


def put(flag, mine, other):
    low = jnp.where(flag, mine, other)
    high = jnp.where(flag, other, mine)
    return jnp.concatenate([low, high], axis=1)


def total(value):
    return jnp.sum(value, axis=1)


def on_device(coupling, amplitude, target, shadow_target):
    row, col = lax.axis_index("row"), lax.axis_index("col")
    x, yh = row >> 1, row & 1
    first = (col & 1) == 0
    z_even = (col & 2) == 0
    low_half = jnp.where(first, (x ^ (x >> 1)) & 1, yh) == 0

    coupling = pltpu.with_memory_space_constraint(coupling, pltpu.HBM)
    g, gs = target, shadow_target
    slope = 1.0 - amplitude * amplitude
    keep = 1.0 - SELF_GAIN * slope

    def send_core(partial, scale):
        mine, other = pick(first, partial * scale)
        return (mine + move(other.astype(WIRE), CORE).astype(F32)).astype(WIRE)

    def send_half(mine, other):
        return (mine + move(other.astype(WIRE), ROW_STEPS[0]).astype(F32)).astype(WIRE)

    half = pick(low_half, (slope * g).astype(BF16))[0]
    half = move(half, HALF_TO_ROWS)
    shadow_partial = shadow(gs.astype(BF16), coupling)

    tops = jnp.stack([jnp.max(jnp.abs(g), axis=1), jnp.max(jnp.abs(gs), axis=1)])
    stats = jnp.concatenate([tops, jnp.stack([total(gs * g), total(gs * (keep * g))])])
    for pairs in SMALL_COL:
        if pairs is SMALL_COL[2]:
            stats, half, shadow_partial = tie(stats, half, shadow_partial)
        other = move(stats, pairs)
        stats = jnp.concatenate(
            [jnp.maximum(stats[:2], other[:2]), stats[2:] + other[2:]]
        )
    tiny = 1e-30
    top = jnp.maximum(stats[0], tiny)[:, None]
    shadow_top = jnp.maximum(stats[1], tiny)[:, None]
    align = stats[2]
    alpha = jnp.clip(stats[2] / stats[3], 1.0, 2.05)
    alpha = jnp.where(jnp.isnan(alpha), 1.4, alpha)
    alpha_c = alpha[:, None]

    block = put(z_even, half, move(half, Z_PAIR))
    left = put(first, block, move(block, CORE))
    shadow_held = send_core(shadow_partial, FIRST_SCALE / shadow_top)
    left, shadow_held = tie(left, shadow_held)
    partial = primary(left, coupling)
    shadow_held = exchange(shadow_held, COL_STEPS[0])
    partial, shadow_held = tie(partial, shadow_held)
    scale = FIRST_SCALE / top
    held = send_half(*pick(low_half, partial * scale))
    shadow_held = exchange(shadow_held, COL_STEPS[1])
    held, shadow_held = tie(held, shadow_held)
    held = exchange(held, ROW_STEPS[1])
    shadow_held = exchange(shadow_held, COL_STEPS[2])
    held, shadow_held = tie(held, shadow_held)
    columns = move(shadow_held, TO_COLS)
    held = exchange(held, ROW_STEPS[2])
    held, columns = tie(held, columns)

    unscale = COUPLE_GAIN / scale

    def first_step(kept, value, product):
        image = kept * value - product.astype(F32) * unscale
        return image, value - alpha_c * image

    g_half, keep_half = pick(low_half, g)[0], pick(low_half, keep)[0]
    slope_half = pick(low_half, slope)[0]
    _, u_half = first_step(keep_half, g_half, held)
    half = move((slope_half * u_half).astype(BF16), HALF_TO_ROWS)
    scale = FIRST_SCALE / shadow_top
    q1 = keep * gs - (COUPLE_GAIN / scale) * slope * columns.astype(F32)
    us = gs - alpha_c * q1

    product = put(low_half, held, move(held, ROW_STEPS[0]))
    shadow_partial = shadow(us.astype(BF16), coupling)
    half, shadow_partial, product = tie(half, shadow_partial, product)

    scale = SECOND_SCALE / shadow_top
    shadow_held = send_core(shadow_partial, scale)
    shadow_held = exchange(shadow_held, COL_STEPS[0])
    block = put(z_even, half, move(half, Z_PAIR))
    p1, u = first_step(keep, g, product)
    dots = jnp.stack(
        [
            total(gs * p1),
            total(us * g),
            total(us * u),
            total(us * p1),
            total(q1 * u),
            total(us * (keep * u)),
        ]
    )
    dots = dots + move(dots, SMALL_COL[0])
    block, shadow_held, dots = tie(block, shadow_held, dots)

    left = put(first, block, move(block, CORE))
    shadow_held = exchange(shadow_held, COL_STEPS[1])
    dots = dots + move(dots, SMALL_COL[1])
    partial = primary(left, coupling)
    partial, shadow_held, dots = tie(partial, shadow_held, dots)

    held = exchange((partial * (SECOND_SCALE / top)).astype(WIRE), ROW_STEPS[0])
    shadow_held = exchange(shadow_held, COL_STEPS[2])
    dots = dots + move(dots, SMALL_COL[2])
    held, shadow_held, dots = tie(held, shadow_held, dots)

    columns = move(shadow_held, TO_COLS)
    last = total(block.astype(F32) * shadow_held.astype(F32)) / scale[:, 0]
    held = exchange(held, ROW_STEPS[1])
    dots = dots + move(dots, SMALL_COL[3])
    for pairs in SMALL_ROW[:2]:
        last = last + move(last, pairs)
    held, columns, dots, last = tie(held, columns, dots, last)

    held = exchange(held, ROW_STEPS[2])
    for pairs in SMALL_ROW[2:]:
        last = last + move(last, pairs)

    p2 = keep * u - held.astype(F32) * (COUPLE_GAIN * top / SECOND_SCALE)
    q2 = keep * us - (COUPLE_GAIN / scale) * slope * columns.astype(F32)
    curve, us_g, us_u, us_p1, q1_u, us_kept = (dots[i] for i in range(6))
    us_p2 = us_kept - COUPLE_GAIN * last
    gs_u = align - alpha * curve
    step = align / curve
    kappa = step / alpha
    rest = 1.0 - kappa
    align_next = (
        rest * rest * align + kappa * rest * (us_g + gs_u) + kappa * kappa * us_u
    )
    blend = align_next / align
    lead = rest + blend
    curve_next = (
        lead * lead * curve + lead * kappa * (us_p1 + q1_u) + kappa * kappa * us_p2
    )
    step_next = align_next / curve_next

    def column(value):
        return value[:, None]

    step, kappa, lead, step_next = map(column, (step, kappa, lead, step_next))
    direction = lead * g + kappa * u
    shadow_direction = lead * gs + kappa * us
    solution = step * g + step_next * direction
    shadow_solution = step * gs + step_next * shadow_direction
    residual = g - step * p1 - step_next * (lead * p1 + kappa * p2)
    shadow_residual = gs - step * q1 - step_next * (lead * q1 + kappa * q2)
    return (solution, shadow_solution, residual, shadow_residual)


def solution(mesh):
    return jax.shard_map(
        on_device,
        mesh=mesh,
        in_specs=(P("row", "col"), P(None, "col"), P(None, "col"), P(None, "col")),
        out_specs=(P(None, "col"), P(None, "col"), P(None, "col"), P(None, "col")),
        check_vma=False,
    )
```

```python
import jax
import jax.numpy as jnp
from jax import lax
from jax.experimental import pallas as pl
from jax.experimental.pallas import tpu as pltpu
from jax.sharding import PartitionSpec as P

SELF_GAIN = 0.5
COUPLE_GAIN = 0.3

F32 = jnp.float32
BF16 = jnp.bfloat16
WIRE = jnp.float16
AXES = ("row", "col")

FIRST_SCALE = 32.0
SECOND_SCALE = 1.0 / 16.0


def split(d):
    row, col = divmod(d, 16)
    return row // 2, row % 2, col // 8, (col // 2) % 4, col % 2


def join(x, yh, yl, z, h):
    return (x * 2 + yh) * 16 + yl * 8 + z * 2 + h


def sends(source_of):
    return [(join(*source_of(*split(d))), d) for d in range(128)]


def flip_x(x, yh, yl, z, h):
    return x ^ 1, yh, yl, z, h


def mirror_x(x, yh, yl, z, h):
    return 3 - x, yh, yl, z, h


def flip_yh(x, yh, yl, z, h):
    return x, yh ^ 1, yl, z, h


def flip_yl(x, yh, yl, z, h):
    return x, yh, yl ^ 1, z, h


def flip_z(x, yh, yl, z, h):
    return x, yh, yl, z ^ 1, h


def mirror_z(x, yh, yl, z, h):
    return x, yh, yl, 3 - z, h


def flip_core(x, yh, yl, z, h):
    return x, yh, yl, z, h ^ 1


def by_core(first, second):
    return sends(lambda *d: (second if d[4] else first)(*d))


STEP = ({0: 2, 1: 1, 2: 0, 3: 3}, {0: 2, 1: 3, 2: 0, 3: 1})


def from_rows(x, yh, yl, z, h):
    xs, yhs = 2 * yl + z // 2, z % 2
    return xs, yhs, yl ^ yh ^ yhs, (z + STEP[h][(x - xs) % 4]) % 4, h


HALF_SOURCE = (
    7, 4, 3, 7, 0, 2, 4, 1, 6, 6, 2, 3, 1, 0, 5, 5,
    7, 0, 2, 5, 0, 6, 5, 7, 6, 2, 4, 3, 1, 4, 3, 1,
    6, 0, 4, 1, 1, 6, 3, 3, 0, 2, 2, 7, 7, 4, 5, 5,
    0, 4, 5, 1, 7, 2, 2, 7, 1, 0, 3, 3, 6, 6, 4, 5,
    0, 6, 3, 7, 7, 4, 4, 1, 1, 0, 5, 3, 6, 2, 2, 5,
    7, 2, 3, 7, 0, 0, 4, 5, 1, 6, 2, 1, 6, 4, 5, 3,
    6, 6, 4, 3, 1, 0, 3, 5, 0, 4, 5, 7, 7, 2, 2, 1,
    0, 4, 5, 7, 7, 2, 2, 1, 6, 0, 3, 5, 1, 6, 4, 3,
)

CORE = sends(flip_core)
TO_COLS = sends(from_rows)
HALF_TO_ROWS = [
    (HALF_SOURCE[d] * 16 + (d // 16) * 2 + d % 2, d) for d in range(128)
]
ROW_STEPS = (
    by_core(flip_x, flip_yh),
    by_core(mirror_x, flip_x),
    by_core(flip_yh, mirror_x),
)
COL_STEPS = (
    by_core(flip_yl, flip_z),
    by_core(flip_z, mirror_z),
    by_core(mirror_z, flip_yl),
)
Z_PAIR = sends(flip_z)
SMALL_COL = (CORE, sends(flip_yl), sends(flip_z), sends(mirror_z))

def fetch(source_ref, held_ref, sems):
    chunks = sems.shape[0]
    size = source_ref.shape[0] // chunks
    copies = []
    for i in range(chunks):
        at = pl.ds(i * size, size)
        copies.append(
            pltpu.make_async_copy(source_ref.at[at], held_ref.at[at], sems.at[i])
        )
        copies[-1].start()
    for i, copy in enumerate(copies):
        copy.wait()
        yield i, pl.ds(i * size, size)


def primary_kernel(left_ref, coupling_ref, out_ref, held_ref, sems):
    for i, at in fetch(coupling_ref, held_ref, sems):
        term = jnp.dot(left_ref[:, at], held_ref[at, :], preferred_element_type=F32)
        if i == 0:
            out_ref[...] = term
        else:
            out_ref[...] += term


def shadow_kernel(left_ref, coupling_ref, out_ref, held_ref, sems):
    for _, at in fetch(coupling_ref, held_ref, sems):
        out_ref[:, at] = lax.dot_general(
            left_ref[...],
            held_ref[at, :],
            (((1,), (1,)), ((), ())),
            preferred_element_type=F32,
        )


def call(kernel, name, left, coupling, width, chunks):
    rows, columns = coupling.shape
    reps = left.shape[0]
    spec = pl.BlockSpec(memory_space=pltpu.VMEM)
    return pl.pallas_call(
        kernel,
        name=name,
        in_specs=[spec, pl.BlockSpec(memory_space=pltpu.HBM)],
        out_specs=spec,
        out_shape=jax.ShapeDtypeStruct((reps, width), F32),
        scratch_shapes=[
            pltpu.VMEM((rows, columns), BF16),
            pltpu.SemaphoreType.DMA((chunks,)),
        ],
        compiler_params=pltpu.CompilerParams(vmem_limit_bytes=24 << 20),
        cost_estimate=pl.CostEstimate(
            flops=2 * reps * rows * columns,
            bytes_accessed=2 * rows * columns,
            transcendentals=0,
        ),
    )(left, coupling)


def primary(left, coupling):
    return call(primary_kernel, "primary", left, coupling, coupling.shape[1], 16)


def shadow(left, coupling):
    return call(shadow_kernel, "shadow", left, coupling, coupling.shape[0], 8)


def half_kernel(offset_ref, left_ref, coupling_ref, out_ref, held_ref, sems):
    width = out_ref.shape[1]
    columns = pl.ds(pl.multiple_of(offset_ref[0], width), width)
    for i, at in fetch(coupling_ref.at[:, columns], held_ref, sems):
        term = jnp.dot(left_ref[:, at], held_ref[at, :], preferred_element_type=F32)
        if i == 0:
            out_ref[...] = term
        else:
            out_ref[...] += term


def primary_half(left, coupling, offset):
    rows, columns = coupling.shape
    reps, width = left.shape[0], columns // 2
    spec = pl.BlockSpec(memory_space=pltpu.VMEM)
    return pl.pallas_call(
        half_kernel,
        name="primary_half",
        in_specs=[
            pl.BlockSpec(memory_space=pltpu.SMEM),
            spec,
            pl.BlockSpec(memory_space=pltpu.HBM),
        ],
        out_specs=spec,
        out_shape=jax.ShapeDtypeStruct((reps, width), F32),
        scratch_shapes=[
            pltpu.VMEM((rows, width), BF16),
            pltpu.SemaphoreType.DMA((16,)),
        ],
        compiler_params=pltpu.CompilerParams(vmem_limit_bytes=16 << 20),
        cost_estimate=pl.CostEstimate(
            flops=2 * reps * rows * width,
            bytes_accessed=2 * rows * width,
            transcendentals=0,
        ),
    )(offset.reshape(1), left, coupling)


def move(value, pairs):
    return lax.ppermute(value, AXES, pairs)


def exchange(held, pairs):
    return (held.astype(F32) + move(held, pairs).astype(F32)).astype(WIRE)


def tie(*values):
    return lax.optimization_barrier(values)


def pick(flag, value):
    width = value.shape[1] // 2
    low, high = value[:, :width], value[:, width:]
    return jnp.where(flag, low, high), jnp.where(flag, high, low)


def put(flag, mine, other):
    low = jnp.where(flag, mine, other)
    high = jnp.where(flag, other, mine)
    return jnp.concatenate([low, high], axis=1)


def total(value):
    return jnp.sum(value, axis=1)


def on_device(coupling, amplitude, target, shadow_target):
    row, col = lax.axis_index("row"), lax.axis_index("col")
    x, yh = row >> 1, row & 1
    first = (col & 1) == 0
    z_even = (col & 2) == 0
    low_half = jnp.where(first, (x ^ (x >> 1)) & 1, yh) == 0

    coupling = pltpu.with_memory_space_constraint(coupling, pltpu.HBM)
    g, gs = target, shadow_target
    slope = 1.0 - amplitude * amplitude
    keep = 1.0 - SELF_GAIN * slope

    def send_core(partial, scale):
        mine, other = pick(first, partial * scale)
        return (mine + move(other.astype(WIRE), CORE).astype(F32)).astype(WIRE)

    half = pick(low_half, (slope * g).astype(BF16))[0]
    half = move(half, HALF_TO_ROWS)
    shadow_partial = shadow(gs.astype(BF16), coupling)

    tops = jnp.stack([jnp.max(jnp.abs(g), axis=1), jnp.max(jnp.abs(gs), axis=1)])
    stats = jnp.concatenate([tops, jnp.stack([total(gs * g), total(gs * (keep * g))])])
    for pairs in SMALL_COL:
        if pairs is SMALL_COL[2]:
            stats, half, shadow_partial = tie(stats, half, shadow_partial)
            block = put(z_even, half, move(half, Z_PAIR))
        if pairs is SMALL_COL[3]:
            stats, block = tie(stats, block)
        other = move(stats, pairs)
        stats = jnp.concatenate(
            [jnp.maximum(stats[:2], other[:2]), stats[2:] + other[2:]]
        )
    tiny = 1e-30
    top = jnp.maximum(stats[0], tiny)[:, None]
    shadow_top = jnp.maximum(stats[1], tiny)[:, None]
    align = stats[2]
    alpha = jnp.clip(stats[2] / stats[3], 1.0, 2.05)
    alpha = jnp.where(jnp.isnan(alpha), 1.4, alpha)
    alpha_c = alpha[:, None]

    left = put(first, block, move(block, CORE))
    shadow_held = send_core(shadow_partial, FIRST_SCALE / shadow_top)
    left, shadow_held = tie(left, shadow_held)
    scale = FIRST_SCALE / top
    offset = jnp.where(low_half, 1024, 0)
    other = primary_half(left, coupling, offset)
    other = move((other * scale).astype(WIRE), ROW_STEPS[0])
    shadow_held = exchange(shadow_held, COL_STEPS[0])
    mine = primary_half(left, coupling, 1024 - offset)
    mine, shadow_held = tie(mine, shadow_held)
    held = (mine * scale + other.astype(F32)).astype(WIRE)
    shadow_held = exchange(shadow_held, COL_STEPS[1])
    held, shadow_held = tie(held, shadow_held)
    held = exchange(held, ROW_STEPS[1])
    shadow_held = exchange(shadow_held, COL_STEPS[2])
    held, shadow_held = tie(held, shadow_held)
    columns = move(shadow_held, TO_COLS)
    held = exchange(held, ROW_STEPS[2])

    unscale = COUPLE_GAIN / scale

    def first_step(kept, value, product):
        image = kept * value - product.astype(F32) * unscale
        return image, value - alpha_c * image

    g_half, keep_half = pick(low_half, g)[0], pick(low_half, keep)[0]
    slope_half = pick(low_half, slope)[0]
    _, u_half = first_step(keep_half, g_half, held)
    u_half = (slope_half * u_half).astype(BF16)
    half = move(u_half, HALF_TO_ROWS)
    columns, _ = tie(columns, u_half)
    scale = FIRST_SCALE / shadow_top
    q1 = keep * gs - (COUPLE_GAIN / scale) * slope * columns.astype(F32)
    us = gs - alpha_c * q1

    shadow_partial = shadow(us.astype(BF16), coupling)
    half, shadow_partial, held = tie(half, shadow_partial, held)
    block = put(z_even, half, move(half, Z_PAIR))
    scale = SECOND_SCALE / shadow_top
    shadow_held = send_core(shadow_partial, scale)
    product = put(low_half, held, move(held, ROW_STEPS[0]))
    block, shadow_held, product = tie(block, shadow_held, product)
    left = put(first, block, move(block, CORE))
    partial = primary(left, coupling)
    shadow_held = exchange(shadow_held, COL_STEPS[0])
    partial, shadow_held = tie(partial, shadow_held)
    held = exchange((partial * (SECOND_SCALE / top)).astype(WIRE), ROW_STEPS[0])
    shadow_held = exchange(shadow_held, COL_STEPS[1])
    held, shadow_held = tie(held, shadow_held)
    held = exchange(held, ROW_STEPS[1])
    shadow_held = exchange(shadow_held, COL_STEPS[2])
    held, shadow_held = tie(held, shadow_held)
    columns = move(shadow_held, TO_COLS)
    held = exchange(held, ROW_STEPS[2])

    p1, u = first_step(keep, g, product)
    p2 = keep * u - held.astype(F32) * (COUPLE_GAIN * top / SECOND_SCALE)
    dots = jnp.stack(
        [
            total(gs * p1),
            total(us * g),
            total(us * u),
            total(us * p1),
            total(q1 * u),
            total(us * p2),
        ]
    )
    for pairs in SMALL_COL:
        if pairs is SMALL_COL[1]:
            dots, columns = tie(dots, columns)
        dots = dots + move(dots, pairs)
    curve, us_g, us_u, us_p1, q1_u, us_p2 = (dots[i] for i in range(6))
    q2 = keep * us - (COUPLE_GAIN / scale) * slope * columns.astype(F32)

    gs_u = align - alpha * curve
    step = align / curve
    kappa = step / alpha
    rest = 1.0 - kappa
    align_next = (
        rest * rest * align + kappa * rest * (us_g + gs_u) + kappa * kappa * us_u
    )
    blend = align_next / align
    lead = rest + blend
    curve_next = (
        lead * lead * curve + lead * kappa * (us_p1 + q1_u) + kappa * kappa * us_p2
    )
    step_next = align_next / curve_next

    def column(value):
        return value[:, None]

    step, kappa, lead, step_next = map(column, (step, kappa, lead, step_next))
    direction = lead * g + kappa * u
    shadow_direction = lead * gs + kappa * us
    solution = step * g + step_next * direction
    shadow_solution = step * gs + step_next * shadow_direction
    residual = g - step * p1 - step_next * (lead * p1 + kappa * p2)
    shadow_residual = gs - step * q1 - step_next * (lead * q1 + kappa * q2)
    return (solution, shadow_solution, residual, shadow_residual)


def solution(mesh):
    return jax.shard_map(
        on_device,
        mesh=mesh,
        in_specs=(P("row", "col"), P(None, "col"), P(None, "col"), P(None, "col")),
        out_specs=(P(None, "col"), P(None, "col"), P(None, "col"), P(None, "col")),
        check_vma=False,
    )
```

```python
import jax
import jax.numpy as jnp
from jax import lax
from jax.experimental import pallas as pl
from jax.experimental.pallas import tpu as pltpu
from jax.sharding import PartitionSpec as P

SELF_GAIN = 0.5
COUPLE_GAIN = 0.3

F32 = jnp.float32
BF16 = jnp.bfloat16
WIRE = jnp.float16
AXES = ("row", "col")

FIRST_SCALE = 32.0
SECOND_SCALE = 1.0 / 16.0


def split(d):
    row, col = divmod(d, 16)
    return row // 2, row % 2, col // 8, (col // 2) % 4, col % 2


def join(x, yh, yl, z, h):
    return (x * 2 + yh) * 16 + yl * 8 + z * 2 + h


def sends(source_of):
    return [(join(*source_of(*split(d))), d) for d in range(128)]


def flip_x(x, yh, yl, z, h):
    return x ^ 1, yh, yl, z, h


def mirror_x(x, yh, yl, z, h):
    return 3 - x, yh, yl, z, h


def flip_yh(x, yh, yl, z, h):
    return x, yh ^ 1, yl, z, h


def flip_yl(x, yh, yl, z, h):
    return x, yh, yl ^ 1, z, h


def flip_z(x, yh, yl, z, h):
    return x, yh, yl, z ^ 1, h


def mirror_z(x, yh, yl, z, h):
    return x, yh, yl, 3 - z, h


def flip_core(x, yh, yl, z, h):
    return x, yh, yl, z, h ^ 1


def by_core(first, second):
    return sends(lambda *d: (second if d[4] else first)(*d))


STEP = ({0: 2, 1: 1, 2: 0, 3: 3}, {0: 2, 1: 3, 2: 0, 3: 1})


def from_rows(x, yh, yl, z, h):
    xs, yhs = 2 * yl + z // 2, z % 2
    return xs, yhs, yl ^ yh ^ yhs, (z + STEP[h][(x - xs) % 4]) % 4, h


HALF_SOURCE = (
    7, 4, 3, 7, 0, 2, 4, 1, 6, 6, 2, 3, 1, 0, 5, 5,
    7, 0, 2, 5, 0, 6, 5, 7, 6, 2, 4, 3, 1, 4, 3, 1,
    6, 0, 4, 1, 1, 6, 3, 3, 0, 2, 2, 7, 7, 4, 5, 5,
    0, 4, 5, 1, 7, 2, 2, 7, 1, 0, 3, 3, 6, 6, 4, 5,
    0, 6, 3, 7, 7, 4, 4, 1, 1, 0, 5, 3, 6, 2, 2, 5,
    7, 2, 3, 7, 0, 0, 4, 5, 1, 6, 2, 1, 6, 4, 5, 3,
    6, 6, 4, 3, 1, 0, 3, 5, 0, 4, 5, 7, 7, 2, 2, 1,
    0, 4, 5, 7, 7, 2, 2, 1, 6, 0, 3, 5, 1, 6, 4, 3,
)

CORE = sends(flip_core)
TO_COLS = sends(from_rows)
HALF_TO_ROWS = [
    (HALF_SOURCE[d] * 16 + (d // 16) * 2 + d % 2, d) for d in range(128)
]
ROW_STEPS = (
    by_core(flip_x, flip_yh),
    by_core(mirror_x, flip_x),
    by_core(flip_yh, mirror_x),
)
COL_STEPS = (
    by_core(flip_yl, flip_z),
    by_core(flip_z, mirror_z),
    by_core(mirror_z, flip_yl),
)
Z_PAIR = sends(flip_z)
SMALL_COL = (CORE, sends(flip_yl), sends(flip_z), sends(mirror_z))

def fetch(source_ref, held_ref, sems):
    chunks = sems.shape[0]
    size = source_ref.shape[0] // chunks
    copies = []
    for i in range(chunks):
        at = pl.ds(i * size, size)
        copies.append(
            pltpu.make_async_copy(source_ref.at[at], held_ref.at[at], sems.at[i])
        )
        copies[-1].start()
    for i, copy in enumerate(copies):
        copy.wait()
        yield i, pl.ds(i * size, size)


def primary_kernel(left_ref, coupling_ref, out_ref, held_ref, sems):
    for i, at in fetch(coupling_ref, held_ref, sems):
        term = jnp.dot(left_ref[:, at], held_ref[at, :], preferred_element_type=F32)
        if i == 0:
            out_ref[...] = term
        else:
            out_ref[...] += term


def shadow_kernel(left_ref, coupling_ref, out_ref, held_ref, sems):
    for _, at in fetch(coupling_ref, held_ref, sems):
        out_ref[:, at] = lax.dot_general(
            left_ref[...],
            held_ref[at, :],
            (((1,), (1,)), ((), ())),
            preferred_element_type=F32,
        )


def call(kernel, name, left, coupling, width, chunks):
    rows, columns = coupling.shape
    reps = left.shape[0]
    spec = pl.BlockSpec(memory_space=pltpu.VMEM)
    return pl.pallas_call(
        kernel,
        name=name,
        in_specs=[spec, pl.BlockSpec(memory_space=pltpu.HBM)],
        out_specs=spec,
        out_shape=jax.ShapeDtypeStruct((reps, width), F32),
        scratch_shapes=[
            pltpu.VMEM((rows, columns), BF16),
            pltpu.SemaphoreType.DMA((chunks,)),
        ],
        compiler_params=pltpu.CompilerParams(vmem_limit_bytes=24 << 20),
        cost_estimate=pl.CostEstimate(
            flops=2 * reps * rows * columns,
            bytes_accessed=2 * rows * columns,
            transcendentals=0,
        ),
    )(left, coupling)


def primary(left, coupling):
    return call(primary_kernel, "primary", left, coupling, coupling.shape[1], 16)


def shadow(left, coupling):
    return call(shadow_kernel, "shadow", left, coupling, coupling.shape[0], 8)


def shadow_rows(left, coupling, start, count):
    columns = coupling.shape[1]
    reps = left.shape[0]
    spec = pl.BlockSpec(memory_space=pltpu.VMEM)

    def kernel(left_ref, coupling_ref, out_ref, held_ref, sems):
        rows = coupling_ref.at[pl.ds(start, count)]
        shadow_kernel(left_ref, rows, out_ref, held_ref, sems)

    return pl.pallas_call(
        kernel,
        name="shadow_rows",
        in_specs=[spec, pl.BlockSpec(memory_space=pltpu.HBM)],
        out_specs=spec,
        out_shape=jax.ShapeDtypeStruct((reps, count), F32),
        scratch_shapes=[
            pltpu.VMEM((count, columns), BF16),
            pltpu.SemaphoreType.DMA((8,)),
        ],
        compiler_params=pltpu.CompilerParams(vmem_limit_bytes=16 << 20),
        cost_estimate=pl.CostEstimate(
            flops=2 * reps * count * columns,
            bytes_accessed=2 * count * columns,
            transcendentals=0,
        ),
    )(left, coupling)


def half_kernel(offset_ref, left_ref, coupling_ref, out_ref, held_ref, sems):
    width = out_ref.shape[1]
    columns = pl.ds(pl.multiple_of(offset_ref[0], width), width)
    for i, at in fetch(coupling_ref.at[:, columns], held_ref, sems):
        term = jnp.dot(left_ref[:, at], held_ref[at, :], preferred_element_type=F32)
        if i == 0:
            out_ref[...] = term
        else:
            out_ref[...] += term


def primary_half(left, coupling, offset):
    rows, columns = coupling.shape
    reps, width = left.shape[0], columns // 2
    spec = pl.BlockSpec(memory_space=pltpu.VMEM)
    return pl.pallas_call(
        half_kernel,
        name="primary_half",
        in_specs=[
            pl.BlockSpec(memory_space=pltpu.SMEM),
            spec,
            pl.BlockSpec(memory_space=pltpu.HBM),
        ],
        out_specs=spec,
        out_shape=jax.ShapeDtypeStruct((reps, width), F32),
        scratch_shapes=[
            pltpu.VMEM((rows, width), BF16),
            pltpu.SemaphoreType.DMA((16,)),
        ],
        compiler_params=pltpu.CompilerParams(vmem_limit_bytes=16 << 20),
        cost_estimate=pl.CostEstimate(
            flops=2 * reps * rows * width,
            bytes_accessed=2 * rows * width,
            transcendentals=0,
        ),
    )(offset.reshape(1), left, coupling)


def move(value, pairs):
    return lax.ppermute(value, AXES, pairs)


def exchange(held, pairs):
    return (held.astype(F32) + move(held, pairs).astype(F32)).astype(WIRE)


def tie(*values):
    return lax.optimization_barrier(values)


def pick(flag, value):
    width = value.shape[1] // 2
    low, high = value[:, :width], value[:, width:]
    return jnp.where(flag, low, high), jnp.where(flag, high, low)


def put(flag, mine, other):
    low = jnp.where(flag, mine, other)
    high = jnp.where(flag, other, mine)
    return jnp.concatenate([low, high], axis=1)


def total(value):
    return jnp.sum(value, axis=1)


def on_device(coupling, amplitude, target, shadow_target):
    row, col = lax.axis_index("row"), lax.axis_index("col")
    x, yh = row >> 1, row & 1
    first = (col & 1) == 0
    z_even = (col & 2) == 0
    low_half = jnp.where(first, (x ^ (x >> 1)) & 1, yh) == 0

    coupling = pltpu.with_memory_space_constraint(coupling, pltpu.HBM)
    g, gs = target, shadow_target
    slope = 1.0 - amplitude * amplitude
    keep = 1.0 - SELF_GAIN * slope

    def send_core(partial, scale):
        low, high = partial
        mine = jnp.where(first, low, high) * scale
        other = jnp.where(first, high, low) * scale
        return (mine + move(other.astype(WIRE), CORE).astype(F32)).astype(WIRE)

    half = pick(low_half, (slope * g).astype(BF16))[0]
    half = move(half, HALF_TO_ROWS)

    tops = jnp.stack([jnp.max(jnp.abs(g), axis=1), jnp.max(jnp.abs(gs), axis=1)])
    stats = jnp.concatenate([tops, jnp.stack([total(gs * g), total(gs * (keep * g))])])

    def widen(stats, pairs):
        other = move(stats, pairs)
        return jnp.concatenate(
            [jnp.maximum(stats[:2], other[:2]), stats[2:] + other[2:]]
        )

    stats = widen(widen(stats, SMALL_COL[0]), SMALL_COL[1])
    shadow_left = gs.astype(BF16)
    low = shadow_rows(shadow_left, coupling, 0, 2048)
    stats, low, shadow_left = tie(stats, low, shadow_left)
    stats = widen(stats, SMALL_COL[2])
    high = shadow_rows(shadow_left, coupling, 2048, 2048)
    stats, high, half = tie(stats, high, half)
    block = put(z_even, half, move(half, Z_PAIR))
    stats = widen(stats, SMALL_COL[3])
    stats, block = tie(stats, block)
    tiny = 1e-30
    top = jnp.maximum(stats[0], tiny)[:, None]
    shadow_top = jnp.maximum(stats[1], tiny)[:, None]
    align = stats[2]
    alpha = jnp.clip(stats[2] / stats[3], 1.0, 2.05)
    alpha = jnp.where(jnp.isnan(alpha), 1.4, alpha)
    alpha_c = alpha[:, None]

    left = put(first, block, move(block, CORE))
    shadow_held = send_core((low, high), FIRST_SCALE / shadow_top)
    left, shadow_held = tie(left, shadow_held)
    scale = FIRST_SCALE / top
    offset = jnp.where(low_half, 1024, 0)
    other = primary_half(left, coupling, offset)
    other = move((other * scale).astype(WIRE), ROW_STEPS[0])
    shadow_held = exchange(shadow_held, COL_STEPS[0])
    mine = primary_half(left, coupling, 1024 - offset)
    mine, shadow_held = tie(mine, shadow_held)
    held = (mine * scale + other.astype(F32)).astype(WIRE)
    shadow_held = exchange(shadow_held, COL_STEPS[1])
    held, shadow_held = tie(held, shadow_held)
    held = exchange(held, ROW_STEPS[1])
    shadow_held = exchange(shadow_held, COL_STEPS[2])
    held, shadow_held = tie(held, shadow_held)
    columns = move(shadow_held, TO_COLS)
    held = exchange(held, ROW_STEPS[2])

    unscale = COUPLE_GAIN / scale

    def first_step(kept, value, product):
        image = kept * value - product.astype(F32) * unscale
        return image, value - alpha_c * image

    g_half, keep_half = pick(low_half, g)[0], pick(low_half, keep)[0]
    slope_half = pick(low_half, slope)[0]
    _, u_half = first_step(keep_half, g_half, held)
    u_half = (slope_half * u_half).astype(BF16)
    half = move(u_half, HALF_TO_ROWS)
    columns, _ = tie(columns, u_half)
    scale = FIRST_SCALE / shadow_top
    q1 = keep * gs - (COUPLE_GAIN / scale) * slope * columns.astype(F32)
    us = gs - alpha_c * q1

    shadow_partial = shadow(us.astype(BF16), coupling)
    half, shadow_partial, held = tie(half, shadow_partial, held)
    block = put(z_even, half, move(half, Z_PAIR))
    scale = SECOND_SCALE / shadow_top
    shadow_held = send_core(jnp.split(shadow_partial, 2, axis=1), scale)
    product = put(low_half, held, move(held, ROW_STEPS[0]))
    block, shadow_held, product = tie(block, shadow_held, product)
    left = put(first, block, move(block, CORE))
    partial = primary(left, coupling)
    shadow_held = exchange(shadow_held, COL_STEPS[0])
    partial, shadow_held = tie(partial, shadow_held)
    held = exchange((partial * (SECOND_SCALE / top)).astype(WIRE), ROW_STEPS[0])
    shadow_held = exchange(shadow_held, COL_STEPS[1])
    held, shadow_held = tie(held, shadow_held)
    held = exchange(held, ROW_STEPS[1])
    shadow_held = exchange(shadow_held, COL_STEPS[2])
    held, shadow_held = tie(held, shadow_held)
    columns = move(shadow_held, TO_COLS)
    held = exchange(held, ROW_STEPS[2])

    p1, u = first_step(keep, g, product)
    p2 = keep * u - held.astype(F32) * (COUPLE_GAIN * top / SECOND_SCALE)
    dots = jnp.stack(
        [
            total(gs * p1),
            total(us * g),
            total(us * u),
            total(us * p1),
            total(q1 * u),
            total(us * p2),
        ]
    )
    for pairs in SMALL_COL:
        if pairs is SMALL_COL[1]:
            dots, columns = tie(dots, columns)
        dots = dots + move(dots, pairs)
    curve, us_g, us_u, us_p1, q1_u, us_p2 = (dots[i] for i in range(6))
    q2 = keep * us - (COUPLE_GAIN / scale) * slope * columns.astype(F32)

    gs_u = align - alpha * curve
    step = align / curve
    kappa = step / alpha
    rest = 1.0 - kappa
    align_next = (
        rest * rest * align + kappa * rest * (us_g + gs_u) + kappa * kappa * us_u
    )
    blend = align_next / align
    lead = rest + blend
    curve_next = (
        lead * lead * curve + lead * kappa * (us_p1 + q1_u) + kappa * kappa * us_p2
    )
    step_next = align_next / curve_next

    def column(value):
        return value[:, None]

    step, kappa, lead, step_next = map(column, (step, kappa, lead, step_next))
    direction = lead * g + kappa * u
    shadow_direction = lead * gs + kappa * us
    solution = step * g + step_next * direction
    shadow_solution = step * gs + step_next * shadow_direction
    residual = g - step * p1 - step_next * (lead * p1 + kappa * p2)
    shadow_residual = gs - step * q1 - step_next * (lead * q1 + kappa * q2)
    return (solution, shadow_solution, residual, shadow_residual)


def solution(mesh):
    return jax.shard_map(
        on_device,
        mesh=mesh,
        in_specs=(P("row", "col"), P(None, "col"), P(None, "col"), P(None, "col")),
        out_specs=(P(None, "col"), P(None, "col"), P(None, "col"), P(None, "col")),
        check_vma=False,
    )
```

```python
import jax
import jax.numpy as jnp
from jax import lax
from jax.experimental import pallas as pl
from jax.experimental.pallas import tpu as pltpu
from jax.sharding import PartitionSpec as P

SELF_GAIN = 0.5
COUPLE_GAIN = 0.3

F32 = jnp.float32
BF16 = jnp.bfloat16
WIRE = jnp.float16
AXES = ("row", "col")

FIRST_SCALE = 32.0
SECOND_SCALE = 1.0 / 16.0


def split(d):
    row, col = divmod(d, 16)
    return row // 2, row % 2, col // 8, (col // 2) % 4, col % 2


def join(x, yh, yl, z, h):
    return (x * 2 + yh) * 16 + yl * 8 + z * 2 + h


def sends(source_of):
    return [(join(*source_of(*split(d))), d) for d in range(128)]


def flip_x(x, yh, yl, z, h):
    return x ^ 1, yh, yl, z, h


def mirror_x(x, yh, yl, z, h):
    return 3 - x, yh, yl, z, h


def flip_yh(x, yh, yl, z, h):
    return x, yh ^ 1, yl, z, h


def flip_yl(x, yh, yl, z, h):
    return x, yh, yl ^ 1, z, h


def flip_z(x, yh, yl, z, h):
    return x, yh, yl, z ^ 1, h


def mirror_z(x, yh, yl, z, h):
    return x, yh, yl, 3 - z, h


def flip_core(x, yh, yl, z, h):
    return x, yh, yl, z, h ^ 1


def by_core(first, second):
    return sends(lambda *d: (second if d[4] else first)(*d))


STEP = ({0: 2, 1: 1, 2: 0, 3: 3}, {0: 2, 1: 3, 2: 0, 3: 1})


def from_rows(x, yh, yl, z, h):
    xs, yhs = 2 * yl + z // 2, z % 2
    return xs, yhs, yl ^ yh ^ yhs, (z + STEP[h][(x - xs) % 4]) % 4, h


HALF_SOURCE = (
    7, 4, 3, 7, 0, 2, 4, 1, 6, 6, 2, 3, 1, 0, 5, 5,
    7, 0, 2, 5, 0, 6, 5, 7, 6, 2, 4, 3, 1, 4, 3, 1,
    6, 0, 4, 1, 1, 6, 3, 3, 0, 2, 2, 7, 7, 4, 5, 5,
    0, 4, 5, 1, 7, 2, 2, 7, 1, 0, 3, 3, 6, 6, 4, 5,
    0, 6, 3, 7, 7, 4, 4, 1, 1, 0, 5, 3, 6, 2, 2, 5,
    7, 2, 3, 7, 0, 0, 4, 5, 1, 6, 2, 1, 6, 4, 5, 3,
    6, 6, 4, 3, 1, 0, 3, 5, 0, 4, 5, 7, 7, 2, 2, 1,
    0, 4, 5, 7, 7, 2, 2, 1, 6, 0, 3, 5, 1, 6, 4, 3,
)

CORE = sends(flip_core)
TO_COLS = sends(from_rows)
HALF_TO_ROWS = [
    (HALF_SOURCE[d] * 16 + (d // 16) * 2 + d % 2, d) for d in range(128)
]
ROW_STEPS = (
    by_core(flip_x, flip_yh),
    by_core(mirror_x, flip_x),
    by_core(flip_yh, mirror_x),
)
COL_STEPS = (
    by_core(flip_yl, flip_z),
    by_core(flip_z, mirror_z),
    by_core(mirror_z, flip_yl),
)
Z_PAIR = sends(flip_z)
SMALL_COL = (CORE, sends(flip_yl), sends(flip_z), sends(mirror_z))

def fetch(source_ref, held_ref, sems):
    chunks = sems.shape[0]
    size = source_ref.shape[0] // chunks
    copies = []
    for i in range(chunks):
        at = pl.ds(i * size, size)
        copies.append(
            pltpu.make_async_copy(source_ref.at[at], held_ref.at[at], sems.at[i])
        )
        copies[-1].start()
    for i, copy in enumerate(copies):
        copy.wait()
        yield i, pl.ds(i * size, size)


def primary_kernel(left_ref, coupling_ref, out_ref, held_ref, sems):
    for i, at in fetch(coupling_ref, held_ref, sems):
        term = jnp.dot(left_ref[:, at], held_ref[at, :], preferred_element_type=F32)
        if i == 0:
            out_ref[...] = term
        else:
            out_ref[...] += term


def shadow_kernel(left_ref, coupling_ref, out_ref, held_ref, sems):
    for _, at in fetch(coupling_ref, held_ref, sems):
        out_ref[:, at] = lax.dot_general(
            left_ref[...],
            held_ref[at, :],
            (((1,), (1,)), ((), ())),
            preferred_element_type=F32,
        )


def call(kernel, name, left, coupling, width, chunks):
    rows, columns = coupling.shape
    reps = left.shape[0]
    spec = pl.BlockSpec(memory_space=pltpu.VMEM)
    return pl.pallas_call(
        kernel,
        name=name,
        in_specs=[spec, pl.BlockSpec(memory_space=pltpu.HBM)],
        out_specs=spec,
        out_shape=jax.ShapeDtypeStruct((reps, width), F32),
        scratch_shapes=[
            pltpu.VMEM((rows, columns), BF16),
            pltpu.SemaphoreType.DMA((chunks,)),
        ],
        compiler_params=pltpu.CompilerParams(vmem_limit_bytes=24 << 20),
        cost_estimate=pl.CostEstimate(
            flops=2 * reps * rows * columns,
            bytes_accessed=2 * rows * columns,
            transcendentals=0,
        ),
    )(left, coupling)


def primary(left, coupling):
    return call(primary_kernel, "primary", left, coupling, coupling.shape[1], 16)


def shadow(left, coupling):
    return call(shadow_kernel, "shadow", left, coupling, coupling.shape[0], 8)


def shadow_rows(left, coupling, start, count):
    columns = coupling.shape[1]
    reps = left.shape[0]
    spec = pl.BlockSpec(memory_space=pltpu.VMEM)

    def kernel(left_ref, coupling_ref, out_ref, held_ref, sems):
        rows = coupling_ref.at[pl.ds(start, count)]
        shadow_kernel(left_ref, rows, out_ref, held_ref, sems)

    return pl.pallas_call(
        kernel,
        name="shadow_rows",
        in_specs=[spec, pl.BlockSpec(memory_space=pltpu.HBM)],
        out_specs=spec,
        out_shape=jax.ShapeDtypeStruct((reps, count), F32),
        scratch_shapes=[
            pltpu.VMEM((count, columns), BF16),
            pltpu.SemaphoreType.DMA((count // 512,)),
        ],
        compiler_params=pltpu.CompilerParams(vmem_limit_bytes=16 << 20),
        cost_estimate=pl.CostEstimate(
            flops=2 * reps * count * columns,
            bytes_accessed=2 * count * columns,
            transcendentals=0,
        ),
    )(left, coupling)


def half_kernel(offset_ref, left_ref, coupling_ref, out_ref, held_ref, sems):
    width = out_ref.shape[1]
    columns = pl.ds(pl.multiple_of(offset_ref[0], width), width)
    for i, at in fetch(coupling_ref.at[:, columns], held_ref, sems):
        term = jnp.dot(left_ref[:, at], held_ref[at, :], preferred_element_type=F32)
        if i == 0:
            out_ref[...] = term
        else:
            out_ref[...] += term


def primary_half(left, coupling, offset):
    rows, columns = coupling.shape
    reps, width = left.shape[0], columns // 2
    spec = pl.BlockSpec(memory_space=pltpu.VMEM)
    return pl.pallas_call(
        half_kernel,
        name="primary_half",
        in_specs=[
            pl.BlockSpec(memory_space=pltpu.SMEM),
            spec,
            pl.BlockSpec(memory_space=pltpu.HBM),
        ],
        out_specs=spec,
        out_shape=jax.ShapeDtypeStruct((reps, width), F32),
        scratch_shapes=[
            pltpu.VMEM((rows, width), BF16),
            pltpu.SemaphoreType.DMA((16,)),
        ],
        compiler_params=pltpu.CompilerParams(vmem_limit_bytes=16 << 20),
        cost_estimate=pl.CostEstimate(
            flops=2 * reps * rows * width,
            bytes_accessed=2 * rows * width,
            transcendentals=0,
        ),
    )(offset.reshape(1), left, coupling)


def move(value, pairs):
    return lax.ppermute(value, AXES, pairs)


def exchange(held, pairs):
    return (held.astype(F32) + move(held, pairs).astype(F32)).astype(WIRE)


def tie(*values):
    return lax.optimization_barrier(values)


def pick(flag, value):
    width = value.shape[1] // 2
    low, high = value[:, :width], value[:, width:]
    return jnp.where(flag, low, high), jnp.where(flag, high, low)


def put(flag, mine, other):
    low = jnp.where(flag, mine, other)
    high = jnp.where(flag, other, mine)
    return jnp.concatenate([low, high], axis=1)


def total(value):
    return jnp.sum(value, axis=1)


def on_device(coupling, amplitude, target, shadow_target):
    row, col = lax.axis_index("row"), lax.axis_index("col")
    x, yh = row >> 1, row & 1
    first = (col & 1) == 0
    z_even = (col & 2) == 0
    low_half = jnp.where(first, (x ^ (x >> 1)) & 1, yh) == 0

    coupling = pltpu.with_memory_space_constraint(coupling, pltpu.HBM)
    g, gs = target, shadow_target
    slope = 1.0 - amplitude * amplitude
    keep = 1.0 - SELF_GAIN * slope

    def send_core(partial, scale):
        low, high = partial
        mine = jnp.where(first, low, high) * scale
        other = jnp.where(first, high, low) * scale
        return (mine + move(other.astype(WIRE), CORE).astype(F32)).astype(WIRE)

    half = pick(low_half, (slope * g).astype(BF16))[0]
    half = move(half, HALF_TO_ROWS)

    tops = jnp.stack([jnp.max(jnp.abs(g), axis=1), jnp.max(jnp.abs(gs), axis=1)])
    stats = jnp.concatenate([tops, jnp.stack([total(gs * g), total(gs * (keep * g))])])

    def widen(stats, pairs):
        other = move(stats, pairs)
        return jnp.concatenate(
            [jnp.maximum(stats[:2], other[:2]), stats[2:] + other[2:]]
        )

    stats = widen(widen(stats, SMALL_COL[0]), SMALL_COL[1])
    shadow_left = gs.astype(BF16)
    low = shadow_rows(shadow_left, coupling, 0, 2048)
    stats, low, shadow_left = tie(stats, low, shadow_left)
    stats = widen(stats, SMALL_COL[2])
    high = shadow_rows(shadow_left, coupling, 2048, 2048)
    stats, high, half = tie(stats, high, half)
    block = put(z_even, half, move(half, Z_PAIR))
    stats = widen(stats, SMALL_COL[3])
    stats, block = tie(stats, block)
    tiny = 1e-30
    top = jnp.maximum(stats[0], tiny)[:, None]
    shadow_top = jnp.maximum(stats[1], tiny)[:, None]
    align = stats[2]
    alpha = jnp.clip(stats[2] / stats[3], 1.0, 2.05)
    alpha = jnp.where(jnp.isnan(alpha), 1.4, alpha)
    alpha_c = alpha[:, None]

    left = put(first, block, move(block, CORE))
    shadow_held = send_core((low, high), FIRST_SCALE / shadow_top)
    left, shadow_held = tie(left, shadow_held)
    scale = FIRST_SCALE / top
    offset = jnp.where(low_half, 1024, 0)
    other = primary_half(left, coupling, offset)
    other = move((other * scale).astype(WIRE), ROW_STEPS[0])
    shadow_held = exchange(shadow_held, COL_STEPS[0])
    mine = primary_half(left, coupling, 1024 - offset)
    mine, shadow_held = tie(mine, shadow_held)
    held = (mine * scale + other.astype(F32)).astype(WIRE)
    shadow_held = exchange(shadow_held, COL_STEPS[1])
    held, shadow_held = tie(held, shadow_held)
    held = exchange(held, ROW_STEPS[1])
    shadow_held = exchange(shadow_held, COL_STEPS[2])
    held, shadow_held = tie(held, shadow_held)
    columns = move(shadow_held, TO_COLS)
    held = exchange(held, ROW_STEPS[2])

    unscale = COUPLE_GAIN / scale

    def first_step(kept, value, product):
        image = kept * value - product.astype(F32) * unscale
        return image, value - alpha_c * image

    g_half, keep_half = pick(low_half, g)[0], pick(low_half, keep)[0]
    slope_half = pick(low_half, slope)[0]
    _, u_half = first_step(keep_half, g_half, held)
    u_half = (slope_half * u_half).astype(BF16)
    half = move(u_half, HALF_TO_ROWS)
    columns, _, late = tie(columns, u_half, held)
    product = put(low_half, late, move(late, ROW_STEPS[0]))
    scale = FIRST_SCALE / shadow_top
    q1 = keep * gs - (COUPLE_GAIN / scale) * slope * columns.astype(F32)
    us = gs - alpha_c * q1

    shadow_partial = shadow(us.astype(BF16), coupling)
    half, shadow_partial, product = tie(half, shadow_partial, product)
    block = put(z_even, half, move(half, Z_PAIR))
    scale = SECOND_SCALE / shadow_top
    shadow_held = send_core(jnp.split(shadow_partial, 2, axis=1), scale)
    block, shadow_held = tie(block, shadow_held)
    left = put(first, block, move(block, CORE))
    partial = primary(left, coupling)
    shadow_held = exchange(shadow_held, COL_STEPS[0])
    partial, shadow_held = tie(partial, shadow_held)
    held = exchange((partial * (SECOND_SCALE / top)).astype(WIRE), ROW_STEPS[0])
    shadow_held = exchange(shadow_held, COL_STEPS[1])
    held, shadow_held = tie(held, shadow_held)
    held = exchange(held, ROW_STEPS[1])
    shadow_held = exchange(shadow_held, COL_STEPS[2])
    held, shadow_held = tie(held, shadow_held)
    columns = move(shadow_held, TO_COLS)
    held = exchange(held, ROW_STEPS[2])

    p1, u = first_step(keep, g, product)
    p2 = keep * u - held.astype(F32) * (COUPLE_GAIN * top / SECOND_SCALE)
    dots = jnp.stack(
        [
            total(gs * p1),
            total(us * g),
            total(us * u),
            total(us * p1),
            total(q1 * u),
            total(us * p2),
        ]
    )
    for pairs in SMALL_COL:
        if pairs is SMALL_COL[1]:
            dots, columns = tie(dots, columns)
        dots = dots + move(dots, pairs)
    curve, us_g, us_u, us_p1, q1_u, us_p2 = (dots[i] for i in range(6))
    q2 = keep * us - (COUPLE_GAIN / scale) * slope * columns.astype(F32)

    gs_u = align - alpha * curve
    step = align / curve
    kappa = step / alpha
    rest = 1.0 - kappa
    align_next = (
        rest * rest * align + kappa * rest * (us_g + gs_u) + kappa * kappa * us_u
    )
    blend = align_next / align
    lead = rest + blend
    curve_next = (
        lead * lead * curve + lead * kappa * (us_p1 + q1_u) + kappa * kappa * us_p2
    )
    step_next = align_next / curve_next

    def column(value):
        return value[:, None]

    step, kappa, lead, step_next = map(column, (step, kappa, lead, step_next))
    direction = lead * g + kappa * u
    shadow_direction = lead * gs + kappa * us
    solution = step * g + step_next * direction
    shadow_solution = step * gs + step_next * shadow_direction
    residual = g - step * p1 - step_next * (lead * p1 + kappa * p2)
    shadow_residual = gs - step * q1 - step_next * (lead * q1 + kappa * q2)
    return (solution, shadow_solution, residual, shadow_residual)


def solution(mesh):
    return jax.shard_map(
        on_device,
        mesh=mesh,
        in_specs=(P("row", "col"), P(None, "col"), P(None, "col"), P(None, "col")),
        out_specs=(P(None, "col"), P(None, "col"), P(None, "col"), P(None, "col")),
        check_vma=False,
    )
```

```python
import jax
import jax.numpy as jnp
from jax import lax
from jax.experimental import pallas as pl
from jax.experimental.pallas import tpu as pltpu
from jax.sharding import PartitionSpec as P

SELF_GAIN = 0.5
COUPLE_GAIN = 0.3

F32 = jnp.float32
BF16 = jnp.bfloat16
WIRE = jnp.float16
AXES = ("row", "col")

FIRST_SCALE = 32.0
SECOND_SCALE = 1.0 / 16.0


def split(d):
    row, col = divmod(d, 16)
    return row // 2, row % 2, col // 8, (col // 2) % 4, col % 2


def join(x, yh, yl, z, h):
    return (x * 2 + yh) * 16 + yl * 8 + z * 2 + h


def sends(source_of):
    return [(join(*source_of(*split(d))), d) for d in range(128)]


def flip_x(x, yh, yl, z, h):
    return x ^ 1, yh, yl, z, h


def mirror_x(x, yh, yl, z, h):
    return 3 - x, yh, yl, z, h


def flip_yh(x, yh, yl, z, h):
    return x, yh ^ 1, yl, z, h


def flip_yl(x, yh, yl, z, h):
    return x, yh, yl ^ 1, z, h


def flip_z(x, yh, yl, z, h):
    return x, yh, yl, z ^ 1, h


def mirror_z(x, yh, yl, z, h):
    return x, yh, yl, 3 - z, h


def flip_core(x, yh, yl, z, h):
    return x, yh, yl, z, h ^ 1


def by_core(first, second):
    return sends(lambda *d: (second if d[4] else first)(*d))


STEP = ({0: 2, 1: 1, 2: 0, 3: 3}, {0: 2, 1: 3, 2: 0, 3: 1})


def from_rows(x, yh, yl, z, h):
    xs, yhs = 2 * yl + z // 2, z % 2
    return xs, yhs, yl ^ yh ^ yhs, (z + STEP[h][(x - xs) % 4]) % 4, h


HALF_SOURCE = (
    7, 4, 3, 7, 0, 2, 4, 1, 6, 6, 2, 3, 1, 0, 5, 5,
    7, 0, 2, 5, 0, 6, 5, 7, 6, 2, 4, 3, 1, 4, 3, 1,
    6, 0, 4, 1, 1, 6, 3, 3, 0, 2, 2, 7, 7, 4, 5, 5,
    0, 4, 5, 1, 7, 2, 2, 7, 1, 0, 3, 3, 6, 6, 4, 5,
    0, 6, 3, 7, 7, 4, 4, 1, 1, 0, 5, 3, 6, 2, 2, 5,
    7, 2, 3, 7, 0, 0, 4, 5, 1, 6, 2, 1, 6, 4, 5, 3,
    6, 6, 4, 3, 1, 0, 3, 5, 0, 4, 5, 7, 7, 2, 2, 1,
    0, 4, 5, 7, 7, 2, 2, 1, 6, 0, 3, 5, 1, 6, 4, 3,
)

CORE = sends(flip_core)
TO_COLS = sends(from_rows)
HALF_TO_ROWS = [
    (HALF_SOURCE[d] * 16 + (d // 16) * 2 + d % 2, d) for d in range(128)
]
ROW_STEPS = (
    by_core(flip_x, flip_yh),
    by_core(mirror_x, flip_x),
    by_core(flip_yh, mirror_x),
)
COL_STEPS = (
    by_core(flip_yl, flip_z),
    by_core(flip_z, mirror_z),
    by_core(mirror_z, flip_yl),
)
Z_PAIR = sends(flip_z)
SMALL_COL = (CORE, sends(flip_yl), sends(flip_z), sends(mirror_z))

def fetch(source_ref, held_ref, sems):
    chunks = sems.shape[0]
    size = source_ref.shape[0] // chunks
    copies = []
    for i in range(chunks):
        at = pl.ds(i * size, size)
        copies.append(
            pltpu.make_async_copy(source_ref.at[at], held_ref.at[at], sems.at[i])
        )
        copies[-1].start()
    for i, copy in enumerate(copies):
        copy.wait()
        yield i, pl.ds(i * size, size)


def primary_kernel(left_ref, coupling_ref, out_ref, held_ref, sems):
    for i, at in fetch(coupling_ref, held_ref, sems):
        term = jnp.dot(left_ref[:, at], held_ref[at, :], preferred_element_type=F32)
        if i == 0:
            out_ref[...] = term
        else:
            out_ref[...] += term


def shadow_kernel(left_ref, coupling_ref, out_ref, held_ref, sems):
    for _, at in fetch(coupling_ref, held_ref, sems):
        out_ref[:, at] = lax.dot_general(
            left_ref[...],
            held_ref[at, :],
            (((1,), (1,)), ((), ())),
            preferred_element_type=F32,
        )


def call(kernel, name, left, coupling, width, chunks):
    rows, columns = coupling.shape
    reps = left.shape[0]
    spec = pl.BlockSpec(memory_space=pltpu.VMEM)
    return pl.pallas_call(
        kernel,
        name=name,
        in_specs=[spec, pl.BlockSpec(memory_space=pltpu.HBM)],
        out_specs=spec,
        out_shape=jax.ShapeDtypeStruct((reps, width), F32),
        scratch_shapes=[
            pltpu.VMEM((rows, columns), BF16),
            pltpu.SemaphoreType.DMA((chunks,)),
        ],
        compiler_params=pltpu.CompilerParams(vmem_limit_bytes=24 << 20),
        cost_estimate=pl.CostEstimate(
            flops=2 * reps * rows * columns,
            bytes_accessed=2 * rows * columns,
            transcendentals=0,
        ),
    )(left, coupling)


def primary(left, coupling):
    return call(primary_kernel, "primary", left, coupling, coupling.shape[1], 16)


def shadow(left, coupling):
    return call(shadow_kernel, "shadow", left, coupling, coupling.shape[0], 8)


def shadow_rows(left, coupling, start, count):
    columns = coupling.shape[1]
    reps = left.shape[0]
    spec = pl.BlockSpec(memory_space=pltpu.VMEM)

    def kernel(left_ref, coupling_ref, out_ref, held_ref, sems):
        rows = coupling_ref.at[pl.ds(start, count)]
        shadow_kernel(left_ref, rows, out_ref, held_ref, sems)

    return pl.pallas_call(
        kernel,
        name="shadow_rows",
        in_specs=[spec, pl.BlockSpec(memory_space=pltpu.HBM)],
        out_specs=spec,
        out_shape=jax.ShapeDtypeStruct((reps, count), F32),
        scratch_shapes=[
            pltpu.VMEM((count, columns), BF16),
            pltpu.SemaphoreType.DMA((count // 512,)),
        ],
        compiler_params=pltpu.CompilerParams(vmem_limit_bytes=16 << 20),
        cost_estimate=pl.CostEstimate(
            flops=2 * reps * count * columns,
            bytes_accessed=2 * count * columns,
            transcendentals=0,
        ),
    )(left, coupling)


def half_kernel(offset_ref, left_ref, coupling_ref, out_ref, held_ref, sems):
    width = out_ref.shape[1]
    columns = pl.ds(pl.multiple_of(offset_ref[0], width), width)
    for i, at in fetch(coupling_ref.at[:, columns], held_ref, sems):
        term = jnp.dot(left_ref[:, at], held_ref[at, :], preferred_element_type=F32)
        if i == 0:
            out_ref[...] = term
        else:
            out_ref[...] += term


def primary_half(left, coupling, offset):
    rows, columns = coupling.shape
    reps, width = left.shape[0], columns // 2
    spec = pl.BlockSpec(memory_space=pltpu.VMEM)
    return pl.pallas_call(
        half_kernel,
        name="primary_half",
        in_specs=[
            pl.BlockSpec(memory_space=pltpu.SMEM),
            spec,
            pl.BlockSpec(memory_space=pltpu.HBM),
        ],
        out_specs=spec,
        out_shape=jax.ShapeDtypeStruct((reps, width), F32),
        scratch_shapes=[
            pltpu.VMEM((rows, width), BF16),
            pltpu.SemaphoreType.DMA((16,)),
        ],
        compiler_params=pltpu.CompilerParams(vmem_limit_bytes=16 << 20),
        cost_estimate=pl.CostEstimate(
            flops=2 * reps * rows * width,
            bytes_accessed=2 * rows * width,
            transcendentals=0,
        ),
    )(offset.reshape(1), left, coupling)


def move(value, pairs):
    return lax.ppermute(value, AXES, pairs)


def exchange(held, pairs):
    return (held.astype(F32) + move(held, pairs).astype(F32)).astype(WIRE)


def tie(*values):
    return lax.optimization_barrier(values)


def pick(flag, value):
    width = value.shape[1] // 2
    low, high = value[:, :width], value[:, width:]
    return jnp.where(flag, low, high), jnp.where(flag, high, low)


def put(flag, mine, other):
    low = jnp.where(flag, mine, other)
    high = jnp.where(flag, other, mine)
    return jnp.concatenate([low, high], axis=1)


def total(value):
    return jnp.sum(value, axis=1)


def on_device(coupling, amplitude, target, shadow_target):
    row, col = lax.axis_index("row"), lax.axis_index("col")
    x, yh = row >> 1, row & 1
    first = (col & 1) == 0
    z_even = (col & 2) == 0
    low_half = jnp.where(first, (x ^ (x >> 1)) & 1, yh) == 0

    coupling = pltpu.with_memory_space_constraint(coupling, pltpu.HBM)
    g, gs = target, shadow_target
    slope = 1.0 - amplitude * amplitude
    keep = 1.0 - SELF_GAIN * slope

    def send_core(partial, scale):
        low, high = partial
        mine = jnp.where(first, low, high) * scale
        other = jnp.where(first, high, low) * scale
        return (mine + move(other.astype(WIRE), CORE).astype(F32)).astype(WIRE)

    half = pick(low_half, (slope * g).astype(BF16))[0]
    half = move(half, HALF_TO_ROWS)

    tops = jnp.stack([jnp.max(jnp.abs(g), axis=1), jnp.max(jnp.abs(gs), axis=1)])
    stats = jnp.concatenate([tops, jnp.stack([total(gs * g), total(gs * (keep * g))])])

    def widen(stats, pairs):
        other = move(stats, pairs)
        return jnp.concatenate(
            [jnp.maximum(stats[:2], other[:2]), stats[2:] + other[2:]]
        )

    stats = widen(widen(stats, SMALL_COL[0]), SMALL_COL[1])
    shadow_left = gs.astype(BF16)
    low = shadow_rows(shadow_left, coupling, 0, 2048)
    stats, low, shadow_left = tie(stats, low, shadow_left)
    stats = widen(stats, SMALL_COL[2])
    high = shadow_rows(shadow_left, coupling, 2048, 2048)
    stats, high, half = tie(stats, high, half)
    block = put(z_even, half, move(half, Z_PAIR))
    stats = widen(stats, SMALL_COL[3])
    stats, block = tie(stats, block)
    tiny = 1e-30
    top = jnp.maximum(stats[0], tiny)[:, None]
    shadow_top = jnp.maximum(stats[1], tiny)[:, None]
    align = stats[2]
    alpha = jnp.clip(stats[2] / stats[3], 1.0, 2.05)
    alpha = jnp.where(jnp.isnan(alpha), 1.4, alpha)
    alpha_c = alpha[:, None]

    left = put(first, block, move(block, CORE))
    shadow_held = send_core((low, high), FIRST_SCALE / shadow_top)
    left, shadow_held = tie(left, shadow_held)
    scale = FIRST_SCALE / top
    offset = jnp.where(low_half, 1024, 0)
    other = primary_half(left, coupling, offset)
    other = move((other * scale).astype(WIRE), ROW_STEPS[0])
    shadow_held = exchange(shadow_held, COL_STEPS[0])
    mine = primary_half(left, coupling, 1024 - offset)
    mine, shadow_held = tie(mine, shadow_held)
    held = (mine * scale + other.astype(F32)).astype(WIRE)
    shadow_held = exchange(shadow_held, COL_STEPS[1])
    held, shadow_held = tie(held, shadow_held)
    held = exchange(held, ROW_STEPS[1])
    shadow_held = exchange(shadow_held, COL_STEPS[2])
    held, shadow_held = tie(held, shadow_held)
    columns = move(shadow_held, TO_COLS)
    held = exchange(held, ROW_STEPS[2])

    unscale = COUPLE_GAIN / scale

    def first_step(kept, value, product):
        image = kept * value - product.astype(F32) * unscale
        return image, value - alpha_c * image

    g_half, keep_half = pick(low_half, g)[0], pick(low_half, keep)[0]
    slope_half = pick(low_half, slope)[0]
    _, u_half = first_step(keep_half, g_half, held)
    u_half = (slope_half * u_half).astype(BF16)
    half = move(u_half, HALF_TO_ROWS)
    columns, _ = tie(columns, u_half)
    scale = FIRST_SCALE / shadow_top
    q1 = keep * gs - (COUPLE_GAIN / scale) * slope * columns.astype(F32)
    us = gs - alpha_c * q1

    shadow_partial = shadow(us.astype(BF16), coupling)
    half, shadow_partial, held = tie(half, shadow_partial, held)
    block = put(z_even, half, move(half, Z_PAIR))
    scale = SECOND_SCALE / shadow_top
    shadow_held = send_core(jnp.split(shadow_partial, 2, axis=1), scale)
    product = put(low_half, held, move(held, ROW_STEPS[0]))
    block, shadow_held, product = tie(block, shadow_held, product)
    left = put(first, block, move(block, CORE))
    partial = primary(left, coupling)
    shadow_held = exchange(shadow_held, COL_STEPS[0])
    partial, shadow_held = tie(partial, shadow_held)
    held = exchange((partial * (SECOND_SCALE / top)).astype(WIRE), ROW_STEPS[0])
    shadow_held = exchange(shadow_held, COL_STEPS[1])
    held, shadow_held = tie(held, shadow_held)
    held = exchange(held, ROW_STEPS[1])
    shadow_held = exchange(shadow_held, COL_STEPS[2])
    held, shadow_held = tie(held, shadow_held)
    columns = move(shadow_held, TO_COLS)
    held = exchange(held, ROW_STEPS[2])

    p1, u = first_step(keep, g, product)
    p2 = keep * u - held.astype(F32) * (COUPLE_GAIN * top / SECOND_SCALE)
    dots = jnp.stack(
        [
            total(gs * p1),
            total(us * g),
            total(us * u),
            total(us * p1),
            total(q1 * u),
            total(us * p2),
        ]
    )
    for pairs in SMALL_COL:
        if pairs is SMALL_COL[2]:
            dots, columns = tie(dots, columns)
        dots = dots + move(dots, pairs)
    curve, us_g, us_u, us_p1, q1_u, us_p2 = (dots[i] for i in range(6))
    q2 = keep * us - (COUPLE_GAIN / scale) * slope * columns.astype(F32)

    gs_u = align - alpha * curve
    step = align / curve
    kappa = step / alpha
    rest = 1.0 - kappa
    align_next = (
        rest * rest * align + kappa * rest * (us_g + gs_u) + kappa * kappa * us_u
    )
    blend = align_next / align
    lead = rest + blend
    curve_next = (
        lead * lead * curve + lead * kappa * (us_p1 + q1_u) + kappa * kappa * us_p2
    )
    step_next = align_next / curve_next

    def column(value):
        return value[:, None]

    step, kappa, lead, step_next = map(column, (step, kappa, lead, step_next))
    direction = lead * g + kappa * u
    shadow_direction = lead * gs + kappa * us
    solution = step * g + step_next * direction
    shadow_solution = step * gs + step_next * shadow_direction
    residual = g - step * p1 - step_next * (lead * p1 + kappa * p2)
    shadow_residual = gs - step * q1 - step_next * (lead * q1 + kappa * q2)
    return (solution, shadow_solution, residual, shadow_residual)


def solution(mesh):
    return jax.shard_map(
        on_device,
        mesh=mesh,
        in_specs=(P("row", "col"), P(None, "col"), P(None, "col"), P(None, "col")),
        out_specs=(P(None, "col"), P(None, "col"), P(None, "col"), P(None, "col")),
        check_vma=False,
    )
```

```python
import jax
import jax.numpy as jnp
from jax import lax
from jax.experimental import pallas as pl
from jax.experimental.pallas import tpu as pltpu
from jax.sharding import PartitionSpec as P

SELF_GAIN = 0.5
COUPLE_GAIN = 0.3

F32 = jnp.float32
BF16 = jnp.bfloat16
WIRE = jnp.float16
AXES = ("row", "col")

FIRST_SCALE = 32.0
SECOND_SCALE = 1.0 / 16.0


def split(d):
    row, col = divmod(d, 16)
    return row // 2, row % 2, col // 8, (col // 2) % 4, col % 2


def join(x, yh, yl, z, h):
    return (x * 2 + yh) * 16 + yl * 8 + z * 2 + h


def sends(source_of):
    return [(join(*source_of(*split(d))), d) for d in range(128)]


def flip_x(x, yh, yl, z, h):
    return x ^ 1, yh, yl, z, h


def mirror_x(x, yh, yl, z, h):
    return 3 - x, yh, yl, z, h


def flip_yh(x, yh, yl, z, h):
    return x, yh ^ 1, yl, z, h


def flip_yl(x, yh, yl, z, h):
    return x, yh, yl ^ 1, z, h


def flip_z(x, yh, yl, z, h):
    return x, yh, yl, z ^ 1, h


def mirror_z(x, yh, yl, z, h):
    return x, yh, yl, 3 - z, h


def flip_core(x, yh, yl, z, h):
    return x, yh, yl, z, h ^ 1


def by_core(first, second):
    return sends(lambda *d: (second if d[4] else first)(*d))


STEP = ({0: 2, 1: 1, 2: 0, 3: 3}, {0: 2, 1: 3, 2: 0, 3: 1})


def from_rows(x, yh, yl, z, h):
    xs, yhs = 2 * yl + z // 2, z % 2
    return xs, yhs, yl ^ yh ^ yhs, (z + STEP[h][(x - xs) % 4]) % 4, h


HALF_SOURCE = (
    7, 4, 3, 7, 0, 2, 4, 1, 6, 6, 2, 3, 1, 0, 5, 5,
    7, 0, 2, 5, 0, 6, 5, 7, 6, 2, 4, 3, 1, 4, 3, 1,
    6, 0, 4, 1, 1, 6, 3, 3, 0, 2, 2, 7, 7, 4, 5, 5,
    0, 4, 5, 1, 7, 2, 2, 7, 1, 0, 3, 3, 6, 6, 4, 5,
    0, 6, 3, 7, 7, 4, 4, 1, 1, 0, 5, 3, 6, 2, 2, 5,
    7, 2, 3, 7, 0, 0, 4, 5, 1, 6, 2, 1, 6, 4, 5, 3,
    6, 6, 4, 3, 1, 0, 3, 5, 0, 4, 5, 7, 7, 2, 2, 1,
    0, 4, 5, 7, 7, 2, 2, 1, 6, 0, 3, 5, 1, 6, 4, 3,
)

CORE = sends(flip_core)
TO_COLS = sends(from_rows)
HALF_TO_ROWS = [
    (HALF_SOURCE[d] * 16 + (d // 16) * 2 + d % 2, d) for d in range(128)
]
ROW_STEPS = (
    by_core(flip_x, flip_yh),
    by_core(mirror_x, flip_x),
    by_core(flip_yh, mirror_x),
)
COL_STEPS = (
    by_core(flip_yl, flip_z),
    by_core(flip_z, mirror_z),
    by_core(mirror_z, flip_yl),
)
Z_PAIR = sends(flip_z)
SMALL_COL = (CORE, sends(flip_yl), sends(flip_z), sends(mirror_z))

def fetch(source_ref, held_ref, sems):
    chunks = sems.shape[0]
    size = source_ref.shape[0] // chunks
    copies = []
    for i in range(chunks):
        at = pl.ds(i * size, size)
        copies.append(
            pltpu.make_async_copy(source_ref.at[at], held_ref.at[at], sems.at[i])
        )
        copies[-1].start()
    for i, copy in enumerate(copies):
        copy.wait()
        yield i, pl.ds(i * size, size)


def primary_kernel(left_ref, coupling_ref, out_ref, held_ref, sems):
    for i, at in fetch(coupling_ref, held_ref, sems):
        term = jnp.dot(left_ref[:, at], held_ref[at, :], preferred_element_type=F32)
        if i == 0:
            out_ref[...] = term
        else:
            out_ref[...] += term


def shadow_kernel(left_ref, coupling_ref, out_ref, held_ref, sems):
    for _, at in fetch(coupling_ref, held_ref, sems):
        out_ref[:, at] = lax.dot_general(
            left_ref[...],
            held_ref[at, :],
            (((1,), (1,)), ((), ())),
            preferred_element_type=F32,
        )


def call(kernel, name, left, coupling, width, chunks):
    rows, columns = coupling.shape
    reps = left.shape[0]
    spec = pl.BlockSpec(memory_space=pltpu.VMEM)
    return pl.pallas_call(
        kernel,
        name=name,
        in_specs=[spec, pl.BlockSpec(memory_space=pltpu.HBM)],
        out_specs=spec,
        out_shape=jax.ShapeDtypeStruct((reps, width), F32),
        scratch_shapes=[
            pltpu.VMEM((rows, columns), BF16),
            pltpu.SemaphoreType.DMA((chunks,)),
        ],
        compiler_params=pltpu.CompilerParams(vmem_limit_bytes=24 << 20),
        cost_estimate=pl.CostEstimate(
            flops=2 * reps * rows * columns,
            bytes_accessed=2 * rows * columns,
            transcendentals=0,
        ),
    )(left, coupling)


def primary(left, coupling):
    return call(primary_kernel, "primary", left, coupling, coupling.shape[1], 16)


def shadow(left, coupling):
    return call(shadow_kernel, "shadow", left, coupling, coupling.shape[0], 8)


def shadow_rows(left, coupling, start, count):
    columns = coupling.shape[1]
    reps = left.shape[0]
    spec = pl.BlockSpec(memory_space=pltpu.VMEM)

    def kernel(left_ref, coupling_ref, out_ref, held_ref, sems):
        rows = coupling_ref.at[pl.ds(start, count)]
        shadow_kernel(left_ref, rows, out_ref, held_ref, sems)

    return pl.pallas_call(
        kernel,
        name="shadow_rows",
        in_specs=[spec, pl.BlockSpec(memory_space=pltpu.HBM)],
        out_specs=spec,
        out_shape=jax.ShapeDtypeStruct((reps, count), F32),
        scratch_shapes=[
            pltpu.VMEM((count, columns), BF16),
            pltpu.SemaphoreType.DMA((count // 512,)),
        ],
        compiler_params=pltpu.CompilerParams(vmem_limit_bytes=16 << 20),
        cost_estimate=pl.CostEstimate(
            flops=2 * reps * count * columns,
            bytes_accessed=2 * count * columns,
            transcendentals=0,
        ),
    )(left, coupling)


def half_kernel(offset_ref, left_ref, coupling_ref, out_ref, held_ref, sems):
    width = out_ref.shape[1]
    columns = pl.ds(pl.multiple_of(offset_ref[0], width), width)
    for i, at in fetch(coupling_ref.at[:, columns], held_ref, sems):
        term = jnp.dot(left_ref[:, at], held_ref[at, :], preferred_element_type=F32)
        if i == 0:
            out_ref[...] = term
        else:
            out_ref[...] += term


def primary_half(left, coupling, offset):
    rows, columns = coupling.shape
    reps, width = left.shape[0], columns // 2
    spec = pl.BlockSpec(memory_space=pltpu.VMEM)
    return pl.pallas_call(
        half_kernel,
        name="primary_half",
        in_specs=[
            pl.BlockSpec(memory_space=pltpu.SMEM),
            spec,
            pl.BlockSpec(memory_space=pltpu.HBM),
        ],
        out_specs=spec,
        out_shape=jax.ShapeDtypeStruct((reps, width), F32),
        scratch_shapes=[
            pltpu.VMEM((rows, width), BF16),
            pltpu.SemaphoreType.DMA((16,)),
        ],
        compiler_params=pltpu.CompilerParams(vmem_limit_bytes=16 << 20),
        cost_estimate=pl.CostEstimate(
            flops=2 * reps * rows * width,
            bytes_accessed=2 * rows * width,
            transcendentals=0,
        ),
    )(offset.reshape(1), left, coupling)


def move(value, pairs):
    return lax.ppermute(value, AXES, pairs)


def exchange(held, pairs):
    return (held.astype(F32) + move(held, pairs).astype(F32)).astype(WIRE)


def tie(*values):
    return lax.optimization_barrier(values)


def pick(flag, value):
    width = value.shape[1] // 2
    low, high = value[:, :width], value[:, width:]
    return jnp.where(flag, low, high), jnp.where(flag, high, low)


def put(flag, mine, other):
    low = jnp.where(flag, mine, other)
    high = jnp.where(flag, other, mine)
    return jnp.concatenate([low, high], axis=1)


def total(value):
    return jnp.sum(value, axis=1)


def on_device(coupling, amplitude, target, shadow_target):
    row, col = lax.axis_index("row"), lax.axis_index("col")
    x, yh = row >> 1, row & 1
    first = (col & 1) == 0
    z_even = (col & 2) == 0
    low_half = jnp.where(first, (x ^ (x >> 1)) & 1, yh) == 0

    coupling = pltpu.with_memory_space_constraint(coupling, pltpu.HBM)
    g, gs = target, shadow_target
    slope = 1.0 - amplitude * amplitude
    keep = 1.0 - SELF_GAIN * slope

    def send_core(partial, scale):
        low, high = partial
        mine = jnp.where(first, low, high) * scale
        other = jnp.where(first, high, low) * scale
        return (mine + move(other.astype(WIRE), CORE).astype(F32)).astype(WIRE)

    half = pick(low_half, (slope * g).astype(BF16))[0]
    half = move(half, HALF_TO_ROWS)

    tops = jnp.stack([jnp.max(jnp.abs(g), axis=1), jnp.max(jnp.abs(gs), axis=1)])
    stats = jnp.concatenate([tops, jnp.stack([total(gs * g), total(gs * (keep * g))])])

    def widen(stats, pairs):
        other = move(stats, pairs)
        return jnp.concatenate(
            [jnp.maximum(stats[:2], other[:2]), stats[2:] + other[2:]]
        )

    stats = widen(widen(stats, SMALL_COL[0]), SMALL_COL[1])
    shadow_left = gs.astype(BF16)
    low = shadow_rows(shadow_left, coupling, 0, 2048)
    stats, low, shadow_left = tie(stats, low, shadow_left)
    stats = widen(stats, SMALL_COL[2])
    high = shadow_rows(shadow_left, coupling, 2048, 2048)
    stats, high, half = tie(stats, high, half)
    block = put(z_even, half, move(half, Z_PAIR))
    stats = widen(stats, SMALL_COL[3])
    stats, block = tie(stats, block)
    tiny = 1e-30
    top = jnp.maximum(stats[0], tiny)[:, None]
    shadow_top = jnp.maximum(stats[1], tiny)[:, None]
    align = stats[2]
    alpha = jnp.clip(stats[2] / stats[3], 1.0, 2.05)
    alpha = jnp.where(jnp.isnan(alpha), 1.4, alpha)
    alpha_c = alpha[:, None]

    left = put(first, block, move(block, CORE))
    shadow_held = send_core((low, high), FIRST_SCALE / shadow_top)
    left, shadow_held = tie(left, shadow_held)
    scale = FIRST_SCALE / top
    offset = jnp.where(low_half, 1024, 0)
    other = primary_half(left, coupling, offset)
    other = move((other * scale).astype(WIRE), ROW_STEPS[0])
    shadow_held = exchange(shadow_held, COL_STEPS[0])
    mine = primary_half(left, coupling, 1024 - offset)
    mine, shadow_held = tie(mine, shadow_held)
    held = (mine * scale + other.astype(F32)).astype(WIRE)
    shadow_held = exchange(shadow_held, COL_STEPS[1])
    held, shadow_held = tie(held, shadow_held)
    held = exchange(held, ROW_STEPS[1])
    shadow_held = exchange(shadow_held, COL_STEPS[2])
    held, shadow_held = tie(held, shadow_held)
    columns = move(shadow_held, TO_COLS)
    held = exchange(held, ROW_STEPS[2])

    unscale = COUPLE_GAIN / scale

    def first_step(kept, value, product):
        image = kept * value - product.astype(F32) * unscale
        return image, value - alpha_c * image

    g_half, keep_half = pick(low_half, g)[0], pick(low_half, keep)[0]
    slope_half = pick(low_half, slope)[0]
    _, u_half = first_step(keep_half, g_half, held)
    u_half = (slope_half * u_half).astype(BF16)
    half = move(u_half, HALF_TO_ROWS)
    columns, _ = tie(columns, u_half)
    scale = FIRST_SCALE / shadow_top
    q1 = keep * gs - (COUPLE_GAIN / scale) * slope * columns.astype(F32)
    us = gs - alpha_c * q1

    shadow_partial = shadow(us.astype(BF16), coupling)
    half, shadow_partial, held = tie(half, shadow_partial, held)
    scale = SECOND_SCALE / shadow_top
    shadow_held = send_core(jnp.split(shadow_partial, 2, axis=1), scale)
    half, shadow_held, held = tie(half, shadow_held, held)
    block = put(z_even, half, move(half, Z_PAIR))
    shadow_held = exchange(shadow_held, COL_STEPS[0])
    product = put(low_half, held, move(held, ROW_STEPS[0]))
    block, shadow_held, product = tie(block, shadow_held, product)
    left = put(first, block, move(block, CORE))
    partial = primary(left, coupling)
    shadow_held = exchange(shadow_held, COL_STEPS[1])
    partial, shadow_held = tie(partial, shadow_held)
    held = exchange((partial * (SECOND_SCALE / top)).astype(WIRE), ROW_STEPS[0])
    shadow_held = exchange(shadow_held, COL_STEPS[2])
    held, shadow_held = tie(held, shadow_held)
    columns = move(shadow_held, TO_COLS)
    held = exchange(held, ROW_STEPS[1])
    held, columns = tie(held, columns)
    held = exchange(held, ROW_STEPS[2])

    p1, u = first_step(keep, g, product)
    p2 = keep * u - held.astype(F32) * (COUPLE_GAIN * top / SECOND_SCALE)
    dots = jnp.stack(
        [
            total(gs * p1),
            total(us * g),
            total(us * u),
            total(us * p1),
            total(q1 * u),
            total(us * p2),
        ]
    )
    for pairs in SMALL_COL:
        dots = dots + move(dots, pairs)
    curve, us_g, us_u, us_p1, q1_u, us_p2 = (dots[i] for i in range(6))
    q2 = keep * us - (COUPLE_GAIN / scale) * slope * columns.astype(F32)

    gs_u = align - alpha * curve
    step = align / curve
    kappa = step / alpha
    rest = 1.0 - kappa
    align_next = (
        rest * rest * align + kappa * rest * (us_g + gs_u) + kappa * kappa * us_u
    )
    blend = align_next / align
    lead = rest + blend
    curve_next = (
        lead * lead * curve + lead * kappa * (us_p1 + q1_u) + kappa * kappa * us_p2
    )
    step_next = align_next / curve_next

    def column(value):
        return value[:, None]

    step, kappa, lead, step_next = map(column, (step, kappa, lead, step_next))
    direction = lead * g + kappa * u
    shadow_direction = lead * gs + kappa * us
    solution = step * g + step_next * direction
    shadow_solution = step * gs + step_next * shadow_direction
    residual = g - step * p1 - step_next * (lead * p1 + kappa * p2)
    shadow_residual = gs - step * q1 - step_next * (lead * q1 + kappa * q2)
    return (solution, shadow_solution, residual, shadow_residual)


def solution(mesh):
    return jax.shard_map(
        on_device,
        mesh=mesh,
        in_specs=(P("row", "col"), P(None, "col"), P(None, "col"), P(None, "col")),
        out_specs=(P(None, "col"), P(None, "col"), P(None, "col"), P(None, "col")),
        check_vma=False,
    )
```

```python
import jax
import jax.numpy as jnp
from jax import lax
from jax.experimental import pallas as pl
from jax.experimental.pallas import tpu as pltpu
from jax.sharding import PartitionSpec as P

SELF_GAIN = 0.5
COUPLE_GAIN = 0.3

F32 = jnp.float32
BF16 = jnp.bfloat16
WIRE = jnp.float16
AXES = ("row", "col")

FIRST_SCALE = 32.0
SECOND_SCALE = 1.0 / 16.0


def split(d):
    row, col = divmod(d, 16)
    return row // 2, row % 2, col // 8, (col // 2) % 4, col % 2


def join(x, yh, yl, z, h):
    return (x * 2 + yh) * 16 + yl * 8 + z * 2 + h


def sends(source_of):
    return [(join(*source_of(*split(d))), d) for d in range(128)]


def flip_x(x, yh, yl, z, h):
    return x ^ 1, yh, yl, z, h


def mirror_x(x, yh, yl, z, h):
    return 3 - x, yh, yl, z, h


def flip_yh(x, yh, yl, z, h):
    return x, yh ^ 1, yl, z, h


def flip_yl(x, yh, yl, z, h):
    return x, yh, yl ^ 1, z, h


def flip_z(x, yh, yl, z, h):
    return x, yh, yl, z ^ 1, h


def mirror_z(x, yh, yl, z, h):
    return x, yh, yl, 3 - z, h


def flip_core(x, yh, yl, z, h):
    return x, yh, yl, z, h ^ 1


def by_core(first, second):
    return sends(lambda *d: (second if d[4] else first)(*d))


STEP = ({0: 2, 1: 1, 2: 0, 3: 3}, {0: 2, 1: 3, 2: 0, 3: 1})


def from_rows(x, yh, yl, z, h):
    xs, yhs = 2 * yl + z // 2, z % 2
    return xs, yhs, yl ^ yh ^ yhs, (z + STEP[h][(x - xs) % 4]) % 4, h


HALF_SOURCE = (
    7, 4, 3, 7, 0, 2, 4, 1, 6, 6, 2, 3, 1, 0, 5, 5,
    7, 0, 2, 5, 0, 6, 5, 7, 6, 2, 4, 3, 1, 4, 3, 1,
    6, 0, 4, 1, 1, 6, 3, 3, 0, 2, 2, 7, 7, 4, 5, 5,
    0, 4, 5, 1, 7, 2, 2, 7, 1, 0, 3, 3, 6, 6, 4, 5,
    0, 6, 3, 7, 7, 4, 4, 1, 1, 0, 5, 3, 6, 2, 2, 5,
    7, 2, 3, 7, 0, 0, 4, 5, 1, 6, 2, 1, 6, 4, 5, 3,
    6, 6, 4, 3, 1, 0, 3, 5, 0, 4, 5, 7, 7, 2, 2, 1,
    0, 4, 5, 7, 7, 2, 2, 1, 6, 0, 3, 5, 1, 6, 4, 3,
)

CORE = sends(flip_core)
TO_COLS = sends(from_rows)
HALF_TO_ROWS = [
    (HALF_SOURCE[d] * 16 + (d // 16) * 2 + d % 2, d) for d in range(128)
]
ROW_STEPS = (
    by_core(flip_x, flip_yh),
    by_core(mirror_x, flip_x),
    by_core(flip_yh, mirror_x),
)
COL_STEPS = (
    by_core(flip_yl, flip_z),
    by_core(flip_z, mirror_z),
    by_core(mirror_z, flip_yl),
)
Z_PAIR = sends(flip_z)
SMALL_COL = (CORE, sends(flip_yl), sends(flip_z), sends(mirror_z))

def fetch(source_ref, held_ref, sems):
    chunks = sems.shape[0]
    size = source_ref.shape[0] // chunks
    copies = []
    for i in range(chunks):
        at = pl.ds(i * size, size)
        copies.append(
            pltpu.make_async_copy(source_ref.at[at], held_ref.at[at], sems.at[i])
        )
        copies[-1].start()
    for i, copy in enumerate(copies):
        copy.wait()
        yield i, pl.ds(i * size, size)


def primary_kernel(left_ref, coupling_ref, out_ref, held_ref, sems):
    for i, at in fetch(coupling_ref, held_ref, sems):
        term = jnp.dot(left_ref[:, at], held_ref[at, :], preferred_element_type=F32)
        if i == 0:
            out_ref[...] = term
        else:
            out_ref[...] += term


def shadow_kernel(left_ref, coupling_ref, out_ref, held_ref, sems):
    for _, at in fetch(coupling_ref, held_ref, sems):
        out_ref[:, at] = lax.dot_general(
            left_ref[...],
            held_ref[at, :],
            (((1,), (1,)), ((), ())),
            preferred_element_type=F32,
        )


def call(kernel, name, left, coupling, width, chunks):
    rows, columns = coupling.shape
    reps = left.shape[0]
    spec = pl.BlockSpec(memory_space=pltpu.VMEM)
    return pl.pallas_call(
        kernel,
        name=name,
        in_specs=[spec, pl.BlockSpec(memory_space=pltpu.HBM)],
        out_specs=spec,
        out_shape=jax.ShapeDtypeStruct((reps, width), F32),
        scratch_shapes=[
            pltpu.VMEM((rows, columns), BF16),
            pltpu.SemaphoreType.DMA((chunks,)),
        ],
        compiler_params=pltpu.CompilerParams(vmem_limit_bytes=24 << 20),
        cost_estimate=pl.CostEstimate(
            flops=2 * reps * rows * columns,
            bytes_accessed=2 * rows * columns,
            transcendentals=0,
        ),
    )(left, coupling)


def primary(left, coupling):
    return call(primary_kernel, "primary", left, coupling, coupling.shape[1], 16)


def shadow(left, coupling):
    return call(shadow_kernel, "shadow", left, coupling, coupling.shape[0], 8)


def shadow_rows(left, coupling, start, count):
    columns = coupling.shape[1]
    reps = left.shape[0]
    spec = pl.BlockSpec(memory_space=pltpu.VMEM)

    def kernel(left_ref, coupling_ref, out_ref, held_ref, sems):
        rows = coupling_ref.at[pl.ds(start, count)]
        shadow_kernel(left_ref, rows, out_ref, held_ref, sems)

    return pl.pallas_call(
        kernel,
        name="shadow_rows",
        in_specs=[spec, pl.BlockSpec(memory_space=pltpu.HBM)],
        out_specs=spec,
        out_shape=jax.ShapeDtypeStruct((reps, count), F32),
        scratch_shapes=[
            pltpu.VMEM((count, columns), BF16),
            pltpu.SemaphoreType.DMA((count // 512,)),
        ],
        compiler_params=pltpu.CompilerParams(vmem_limit_bytes=16 << 20),
        cost_estimate=pl.CostEstimate(
            flops=2 * reps * count * columns,
            bytes_accessed=2 * count * columns,
            transcendentals=0,
        ),
    )(left, coupling)


def half_kernel(offset_ref, left_ref, coupling_ref, out_ref, held_ref, sems):
    width = out_ref.shape[1]
    columns = pl.ds(pl.multiple_of(offset_ref[0], width), width)
    for i, at in fetch(coupling_ref.at[:, columns], held_ref, sems):
        term = jnp.dot(left_ref[:, at], held_ref[at, :], preferred_element_type=F32)
        if i == 0:
            out_ref[...] = term
        else:
            out_ref[...] += term


def primary_half(left, coupling, offset):
    rows, columns = coupling.shape
    reps, width = left.shape[0], columns // 2
    spec = pl.BlockSpec(memory_space=pltpu.VMEM)
    return pl.pallas_call(
        half_kernel,
        name="primary_half",
        in_specs=[
            pl.BlockSpec(memory_space=pltpu.SMEM),
            spec,
            pl.BlockSpec(memory_space=pltpu.HBM),
        ],
        out_specs=spec,
        out_shape=jax.ShapeDtypeStruct((reps, width), F32),
        scratch_shapes=[
            pltpu.VMEM((rows, width), BF16),
            pltpu.SemaphoreType.DMA((16,)),
        ],
        compiler_params=pltpu.CompilerParams(vmem_limit_bytes=16 << 20),
        cost_estimate=pl.CostEstimate(
            flops=2 * reps * rows * width,
            bytes_accessed=2 * rows * width,
            transcendentals=0,
        ),
    )(offset.reshape(1), left, coupling)


def move(value, pairs):
    return lax.ppermute(value, AXES, pairs)


def exchange(held, pairs):
    return (held.astype(F32) + move(held, pairs).astype(F32)).astype(WIRE)


def tie(*values):
    return lax.optimization_barrier(values)


def pick(flag, value):
    width = value.shape[1] // 2
    low, high = value[:, :width], value[:, width:]
    return jnp.where(flag, low, high), jnp.where(flag, high, low)


def put(flag, mine, other):
    low = jnp.where(flag, mine, other)
    high = jnp.where(flag, other, mine)
    return jnp.concatenate([low, high], axis=1)


def total(value):
    return jnp.sum(value, axis=1)


def on_device(coupling, amplitude, target, shadow_target):
    row, col = lax.axis_index("row"), lax.axis_index("col")
    x, yh = row >> 1, row & 1
    first = (col & 1) == 0
    z_even = (col & 2) == 0
    low_half = jnp.where(first, (x ^ (x >> 1)) & 1, yh) == 0

    coupling = pltpu.with_memory_space_constraint(coupling, pltpu.HBM)
    g, gs = target, shadow_target
    slope = 1.0 - amplitude * amplitude
    keep = 1.0 - SELF_GAIN * slope

    def send_core(partial, scale):
        low, high = partial
        mine = jnp.where(first, low, high) * scale
        other = jnp.where(first, high, low) * scale
        return (mine + move(other.astype(WIRE), CORE).astype(F32)).astype(WIRE)

    half = pick(low_half, (slope * g).astype(BF16))[0]
    half = move(half, HALF_TO_ROWS)

    tops = jnp.stack([jnp.max(jnp.abs(g), axis=1), jnp.max(jnp.abs(gs), axis=1)])
    stats = jnp.concatenate([tops, jnp.stack([total(gs * g), total(gs * (keep * g))])])

    def widen(stats, pairs):
        other = move(stats, pairs)
        return jnp.concatenate(
            [jnp.maximum(stats[:2], other[:2]), stats[2:] + other[2:]]
        )

    stats = widen(widen(stats, SMALL_COL[0]), SMALL_COL[1])
    shadow_left = gs.astype(BF16)
    low = shadow_rows(shadow_left, coupling, 0, 2048)
    stats, low, shadow_left = tie(stats, low, shadow_left)
    stats = widen(stats, SMALL_COL[2])
    high = shadow_rows(shadow_left, coupling, 2048, 2048)
    stats, high, half = tie(stats, high, half)
    block = put(z_even, half, move(half, Z_PAIR))
    stats = widen(stats, SMALL_COL[3])
    stats, block = tie(stats, block)
    tiny = 1e-30
    top = jnp.maximum(stats[0], tiny)[:, None]
    shadow_top = jnp.maximum(stats[1], tiny)[:, None]
    align = stats[2]
    alpha = jnp.clip(stats[2] / stats[3], 1.0, 2.05)
    alpha = jnp.where(jnp.isnan(alpha), 1.4, alpha)
    alpha_c = alpha[:, None]

    left = put(first, block, move(block, CORE))
    shadow_held = send_core((low, high), FIRST_SCALE / shadow_top)
    left, shadow_held = tie(left, shadow_held)
    scale = FIRST_SCALE / top
    offset = jnp.where(low_half, 1024, 0)
    other = primary_half(left, coupling, offset)
    other = move((other * scale).astype(WIRE), ROW_STEPS[0])
    shadow_held = exchange(shadow_held, COL_STEPS[0])
    mine = primary_half(left, coupling, 1024 - offset)
    mine, shadow_held = tie(mine, shadow_held)
    held = (mine * scale + other.astype(F32)).astype(WIRE)
    shadow_held = exchange(shadow_held, COL_STEPS[1])
    held, shadow_held = tie(held, shadow_held)
    held = exchange(held, ROW_STEPS[1])
    shadow_held = exchange(shadow_held, COL_STEPS[2])
    held, shadow_held = tie(held, shadow_held)
    columns = move(shadow_held, TO_COLS)
    held = exchange(held, ROW_STEPS[2])

    unscale = COUPLE_GAIN / scale

    def first_step(kept, value, product):
        image = kept * value - product.astype(F32) * unscale
        return image, value - alpha_c * image

    g_half, keep_half = pick(low_half, g)[0], pick(low_half, keep)[0]
    slope_half = pick(low_half, slope)[0]
    _, u_half = first_step(keep_half, g_half, held)
    u_half = (slope_half * u_half).astype(BF16)
    half = move(u_half, HALF_TO_ROWS)
    columns, _ = tie(columns, u_half)
    scale = FIRST_SCALE / shadow_top
    q1 = keep * gs - (COUPLE_GAIN / scale) * slope * columns.astype(F32)
    us = gs - alpha_c * q1

    shadow_partial = shadow(us.astype(BF16), coupling)
    half, shadow_partial, held = tie(half, shadow_partial, held)
    block = put(z_even, half, move(half, Z_PAIR))
    scale = SECOND_SCALE / shadow_top
    shadow_held = send_core(jnp.split(shadow_partial, 2, axis=1), scale)
    block, shadow_held, held = tie(block, shadow_held, held)
    left = put(first, block, move(block, CORE))
    partial = primary(left, coupling)
    shadow_held = exchange(shadow_held, COL_STEPS[0])
    product = put(low_half, held, move(held, ROW_STEPS[0]))
    partial, shadow_held, product = tie(partial, shadow_held, product)
    held = exchange((partial * (SECOND_SCALE / top)).astype(WIRE), ROW_STEPS[0])
    shadow_held = exchange(shadow_held, COL_STEPS[1])
    held, shadow_held = tie(held, shadow_held)
    held = exchange(held, ROW_STEPS[1])
    shadow_held = exchange(shadow_held, COL_STEPS[2])
    held, shadow_held = tie(held, shadow_held)
    columns = move(shadow_held, TO_COLS)
    held = exchange(held, ROW_STEPS[2])

    p1, u = first_step(keep, g, product)
    p2 = keep * u - held.astype(F32) * (COUPLE_GAIN * top / SECOND_SCALE)
    dots = jnp.stack(
        [
            total(gs * p1),
            total(us * g),
            total(us * u),
            total(us * p1),
            total(q1 * u),
            total(us * p2),
        ]
    )
    for pairs in SMALL_COL:
        if pairs is SMALL_COL[2]:
            dots, columns = tie(dots, columns)
        dots = dots + move(dots, pairs)
    curve, us_g, us_u, us_p1, q1_u, us_p2 = (dots[i] for i in range(6))
    q2 = keep * us - (COUPLE_GAIN / scale) * slope * columns.astype(F32)

    gs_u = align - alpha * curve
    step = align / curve
    kappa = step / alpha
    rest = 1.0 - kappa
    align_next = (
        rest * rest * align + kappa * rest * (us_g + gs_u) + kappa * kappa * us_u
    )
    blend = align_next / align
    lead = rest + blend
    curve_next = (
        lead * lead * curve + lead * kappa * (us_p1 + q1_u) + kappa * kappa * us_p2
    )
    step_next = align_next / curve_next

    def column(value):
        return value[:, None]

    step, kappa, lead, step_next = map(column, (step, kappa, lead, step_next))
    direction = lead * g + kappa * u
    shadow_direction = lead * gs + kappa * us
    solution = step * g + step_next * direction
    shadow_solution = step * gs + step_next * shadow_direction
    residual = g - step * p1 - step_next * (lead * p1 + kappa * p2)
    shadow_residual = gs - step * q1 - step_next * (lead * q1 + kappa * q2)
    return (solution, shadow_solution, residual, shadow_residual)


def solution(mesh):
    return jax.shard_map(
        on_device,
        mesh=mesh,
        in_specs=(P("row", "col"), P(None, "col"), P(None, "col"), P(None, "col")),
        out_specs=(P(None, "col"), P(None, "col"), P(None, "col"), P(None, "col")),
        check_vma=False,
    )
```

```python
import jax
import jax.numpy as jnp
from jax import lax
from jax.experimental import pallas as pl
from jax.experimental.pallas import tpu as pltpu
from jax.sharding import PartitionSpec as P

SELF_GAIN = 0.5
COUPLE_GAIN = 0.3

F32 = jnp.float32
BF16 = jnp.bfloat16
WIRE = jnp.float16
AXES = ("row", "col")

FIRST_SCALE = 32.0
SECOND_SCALE = 1.0 / 16.0


def split(d):
    row, col = divmod(d, 16)
    return row // 2, row % 2, col // 8, (col // 2) % 4, col % 2


def join(x, yh, yl, z, h):
    return (x * 2 + yh) * 16 + yl * 8 + z * 2 + h


def sends(source_of):
    return [(join(*source_of(*split(d))), d) for d in range(128)]


def flip_x(x, yh, yl, z, h):
    return x ^ 1, yh, yl, z, h


def mirror_x(x, yh, yl, z, h):
    return 3 - x, yh, yl, z, h


def flip_yh(x, yh, yl, z, h):
    return x, yh ^ 1, yl, z, h


def flip_yl(x, yh, yl, z, h):
    return x, yh, yl ^ 1, z, h


def flip_z(x, yh, yl, z, h):
    return x, yh, yl, z ^ 1, h


def mirror_z(x, yh, yl, z, h):
    return x, yh, yl, 3 - z, h


def flip_core(x, yh, yl, z, h):
    return x, yh, yl, z, h ^ 1


def by_core(first, second):
    return sends(lambda *d: (second if d[4] else first)(*d))


STEP = ({0: 2, 1: 1, 2: 0, 3: 3}, {0: 2, 1: 3, 2: 0, 3: 1})


def from_rows(x, yh, yl, z, h):
    xs, yhs = 2 * yl + z // 2, z % 2
    return xs, yhs, yl ^ yh ^ yhs, (z + STEP[h][(x - xs) % 4]) % 4, h


HALF_SOURCE = (
    7, 4, 3, 7, 0, 2, 4, 1, 6, 6, 2, 3, 1, 0, 5, 5,
    7, 0, 2, 5, 0, 6, 5, 7, 6, 2, 4, 3, 1, 4, 3, 1,
    6, 0, 4, 1, 1, 6, 3, 3, 0, 2, 2, 7, 7, 4, 5, 5,
    0, 4, 5, 1, 7, 2, 2, 7, 1, 0, 3, 3, 6, 6, 4, 5,
    0, 6, 3, 7, 7, 4, 4, 1, 1, 0, 5, 3, 6, 2, 2, 5,
    7, 2, 3, 7, 0, 0, 4, 5, 1, 6, 2, 1, 6, 4, 5, 3,
    6, 6, 4, 3, 1, 0, 3, 5, 0, 4, 5, 7, 7, 2, 2, 1,
    0, 4, 5, 7, 7, 2, 2, 1, 6, 0, 3, 5, 1, 6, 4, 3,
)

CORE = sends(flip_core)
TO_COLS = sends(from_rows)
HALF_TO_ROWS = [
    (HALF_SOURCE[d] * 16 + (d // 16) * 2 + d % 2, d) for d in range(128)
]
ROW_STEPS = (
    by_core(flip_x, flip_yh),
    by_core(mirror_x, flip_x),
    by_core(flip_yh, mirror_x),
)
COL_STEPS = (
    by_core(flip_yl, flip_z),
    by_core(flip_z, mirror_z),
    by_core(mirror_z, flip_yl),
)
Z_PAIR = sends(flip_z)
SMALL_COL = (CORE, sends(flip_yl), sends(flip_z), sends(mirror_z))

def fetch(source_ref, held_ref, sems):
    chunks = sems.shape[0]
    size = source_ref.shape[0] // chunks
    copies = []
    for i in range(chunks):
        at = pl.ds(i * size, size)
        copies.append(
            pltpu.make_async_copy(source_ref.at[at], held_ref.at[at], sems.at[i])
        )
        copies[-1].start()
    for i, copy in enumerate(copies):
        copy.wait()
        yield i, pl.ds(i * size, size)


def primary_kernel(left_ref, coupling_ref, out_ref, held_ref, sems):
    for i, at in fetch(coupling_ref, held_ref, sems):
        term = jnp.dot(left_ref[:, at], held_ref[at, :], preferred_element_type=F32)
        if i == 0:
            out_ref[...] = term
        else:
            out_ref[...] += term


def shadow_kernel(left_ref, coupling_ref, out_ref, held_ref, sems):
    for _, at in fetch(coupling_ref, held_ref, sems):
        out_ref[:, at] = lax.dot_general(
            left_ref[...],
            held_ref[at, :],
            (((1,), (1,)), ((), ())),
            preferred_element_type=F32,
        )


def call(kernel, name, left, coupling, width, chunks):
    rows, columns = coupling.shape
    reps = left.shape[0]
    spec = pl.BlockSpec(memory_space=pltpu.VMEM)
    return pl.pallas_call(
        kernel,
        name=name,
        in_specs=[spec, pl.BlockSpec(memory_space=pltpu.HBM)],
        out_specs=spec,
        out_shape=jax.ShapeDtypeStruct((reps, width), F32),
        scratch_shapes=[
            pltpu.VMEM((rows, columns), BF16),
            pltpu.SemaphoreType.DMA((chunks,)),
        ],
        compiler_params=pltpu.CompilerParams(vmem_limit_bytes=24 << 20),
        cost_estimate=pl.CostEstimate(
            flops=2 * reps * rows * columns,
            bytes_accessed=2 * rows * columns,
            transcendentals=0,
        ),
    )(left, coupling)


def primary(left, coupling):
    return call(primary_kernel, "primary", left, coupling, coupling.shape[1], 16)


def shadow(left, coupling):
    return call(shadow_kernel, "shadow", left, coupling, coupling.shape[0], 8)


def shadow_rows(left, coupling, start, count):
    columns = coupling.shape[1]
    reps = left.shape[0]
    spec = pl.BlockSpec(memory_space=pltpu.VMEM)

    def kernel(left_ref, coupling_ref, out_ref, held_ref, sems):
        rows = coupling_ref.at[pl.ds(start, count)]
        shadow_kernel(left_ref, rows, out_ref, held_ref, sems)

    return pl.pallas_call(
        kernel,
        name="shadow_rows",
        in_specs=[spec, pl.BlockSpec(memory_space=pltpu.HBM)],
        out_specs=spec,
        out_shape=jax.ShapeDtypeStruct((reps, count), F32),
        scratch_shapes=[
            pltpu.VMEM((count, columns), BF16),
            pltpu.SemaphoreType.DMA((count // 512,)),
        ],
        compiler_params=pltpu.CompilerParams(vmem_limit_bytes=16 << 20),
        cost_estimate=pl.CostEstimate(
            flops=2 * reps * count * columns,
            bytes_accessed=2 * count * columns,
            transcendentals=0,
        ),
    )(left, coupling)


def half_kernel(offset_ref, left_ref, coupling_ref, out_ref, held_ref, sems):
    width = out_ref.shape[1]
    columns = pl.ds(pl.multiple_of(offset_ref[0], width), width)
    for i, at in fetch(coupling_ref.at[:, columns], held_ref, sems):
        term = jnp.dot(left_ref[:, at], held_ref[at, :], preferred_element_type=F32)
        if i == 0:
            out_ref[...] = term
        else:
            out_ref[...] += term


def primary_half(left, coupling, offset):
    rows, columns = coupling.shape
    reps, width = left.shape[0], columns // 2
    spec = pl.BlockSpec(memory_space=pltpu.VMEM)
    return pl.pallas_call(
        half_kernel,
        name="primary_half",
        in_specs=[
            pl.BlockSpec(memory_space=pltpu.SMEM),
            spec,
            pl.BlockSpec(memory_space=pltpu.HBM),
        ],
        out_specs=spec,
        out_shape=jax.ShapeDtypeStruct((reps, width), F32),
        scratch_shapes=[
            pltpu.VMEM((rows, width), BF16),
            pltpu.SemaphoreType.DMA((16,)),
        ],
        compiler_params=pltpu.CompilerParams(vmem_limit_bytes=16 << 20),
        cost_estimate=pl.CostEstimate(
            flops=2 * reps * rows * width,
            bytes_accessed=2 * rows * width,
            transcendentals=0,
        ),
    )(offset.reshape(1), left, coupling)


def move(value, pairs):
    return lax.ppermute(value, AXES, pairs)


def exchange(held, pairs):
    return (held.astype(F32) + move(held, pairs).astype(F32)).astype(WIRE)


def tie(*values):
    return lax.optimization_barrier(values)


def pick(flag, value):
    width = value.shape[1] // 2
    low, high = value[:, :width], value[:, width:]
    return jnp.where(flag, low, high), jnp.where(flag, high, low)


def put(flag, mine, other):
    low = jnp.where(flag, mine, other)
    high = jnp.where(flag, other, mine)
    return jnp.concatenate([low, high], axis=1)


def total(value):
    return jnp.sum(value, axis=1)


def on_device(coupling, amplitude, target, shadow_target):
    row, col = lax.axis_index("row"), lax.axis_index("col")
    x, yh = row >> 1, row & 1
    first = (col & 1) == 0
    z_even = (col & 2) == 0
    low_half = jnp.where(first, (x ^ (x >> 1)) & 1, yh) == 0

    coupling = pltpu.with_memory_space_constraint(coupling, pltpu.HBM)
    g, gs = target, shadow_target
    slope = 1.0 - amplitude * amplitude
    keep = 1.0 - SELF_GAIN * slope

    def send_core(partial, scale):
        low, high = partial
        mine = jnp.where(first, low, high) * scale
        other = jnp.where(first, high, low) * scale
        return (mine + move(other.astype(WIRE), CORE).astype(F32)).astype(WIRE)

    half = pick(low_half, (slope * g).astype(BF16))[0]
    half = move(half, HALF_TO_ROWS)

    tops = jnp.stack([jnp.max(jnp.abs(g), axis=1), jnp.max(jnp.abs(gs), axis=1)])
    stats = jnp.concatenate([tops, jnp.stack([total(gs * g), total(gs * (keep * g))])])

    def widen(stats, pairs):
        other = move(stats, pairs)
        return jnp.concatenate(
            [jnp.maximum(stats[:2], other[:2]), stats[2:] + other[2:]]
        )

    stats = widen(widen(stats, SMALL_COL[0]), SMALL_COL[1])
    shadow_left = gs.astype(BF16)
    low = shadow_rows(shadow_left, coupling, 0, 2048)
    stats, low, shadow_left = tie(stats, low, shadow_left)
    stats = widen(stats, SMALL_COL[2])
    high = shadow_rows(shadow_left, coupling, 2048, 2048)
    stats, high, half = tie(stats, high, half)
    block = put(z_even, half, move(half, Z_PAIR))
    stats = widen(stats, SMALL_COL[3])
    stats, block = tie(stats, block)
    tiny = 1e-30
    top = jnp.maximum(stats[0], tiny)[:, None]
    shadow_top = jnp.maximum(stats[1], tiny)[:, None]
    align = stats[2]
    alpha = jnp.clip(stats[2] / stats[3], 1.0, 2.05)
    alpha = jnp.where(jnp.isnan(alpha), 1.4, alpha)
    alpha_c = alpha[:, None]

    left = put(first, block, move(block, CORE))
    shadow_held = send_core((low, high), FIRST_SCALE / shadow_top)
    left, shadow_held = tie(left, shadow_held)
    scale = FIRST_SCALE / top
    offset = jnp.where(low_half, 1024, 0)
    other = primary_half(left, coupling, offset)
    other = move((other * scale).astype(WIRE), ROW_STEPS[0])
    shadow_held = exchange(shadow_held, COL_STEPS[0])
    mine = primary_half(left, coupling, 1024 - offset)
    mine, shadow_held = tie(mine, shadow_held)
    held = (mine * scale + other.astype(F32)).astype(WIRE)
    shadow_held = exchange(shadow_held, COL_STEPS[1])
    held, shadow_held = tie(held, shadow_held)
    held = exchange(held, ROW_STEPS[1])
    shadow_held = exchange(shadow_held, COL_STEPS[2])
    held, shadow_held = tie(held, shadow_held)
    columns = move(shadow_held, TO_COLS)
    held = exchange(held, ROW_STEPS[2])

    unscale = COUPLE_GAIN / scale

    def first_step(kept, value, product):
        image = kept * value - product.astype(F32) * unscale
        return image, value - alpha_c * image

    g_half, keep_half = pick(low_half, g)[0], pick(low_half, keep)[0]
    slope_half = pick(low_half, slope)[0]
    _, u_half = first_step(keep_half, g_half, held)
    u_half = (slope_half * u_half).astype(BF16)
    half = move(u_half, HALF_TO_ROWS)
    columns, _ = tie(columns, u_half)
    scale = FIRST_SCALE / shadow_top
    q1 = keep * gs - (COUPLE_GAIN / scale) * slope * columns.astype(F32)
    us = gs - alpha_c * q1

    shadow_partial = shadow(us.astype(BF16), coupling)
    half, shadow_partial, held = tie(half, shadow_partial, held)
    block = put(z_even, half, move(half, Z_PAIR))
    scale = SECOND_SCALE / shadow_top
    shadow_held = send_core(jnp.split(shadow_partial, 2, axis=1), scale)
    product = put(low_half, held, move(held, ROW_STEPS[0]))
    block, shadow_held, product = tie(block, shadow_held, product)
    left = put(first, block, move(block, CORE))
    partial = primary(left, coupling)
    shadow_held = exchange(shadow_held, COL_STEPS[0])
    partial, shadow_held = tie(partial, shadow_held)
    held = exchange((partial * (SECOND_SCALE / top)).astype(WIRE), ROW_STEPS[0])
    shadow_held = exchange(shadow_held, COL_STEPS[1])
    held, shadow_held = tie(held, shadow_held)
    held = exchange(held, ROW_STEPS[1])
    shadow_held = exchange(shadow_held, COL_STEPS[2])
    held, shadow_held = tie(held, shadow_held)
    columns = move(shadow_held, TO_COLS)
    held = exchange(held, ROW_STEPS[2])

    p1, u = first_step(keep, g, product)
    p2 = keep * u - held.astype(F32) * (COUPLE_GAIN * top / SECOND_SCALE)
    dots = jnp.stack(
        [
            total(gs * p1),
            total(us * g),
            total(us * u),
            total(us * p1),
            total(q1 * u),
            total(us * p2),
        ]
    )
    for pairs in SMALL_COL:
        if pairs is SMALL_COL[3]:
            dots, columns = tie(dots, columns)
        dots = dots + move(dots, pairs)
    curve, us_g, us_u, us_p1, q1_u, us_p2 = (dots[i] for i in range(6))
    q2 = keep * us - (COUPLE_GAIN / scale) * slope * columns.astype(F32)

    gs_u = align - alpha * curve
    step = align / curve
    kappa = step / alpha
    rest = 1.0 - kappa
    align_next = (
        rest * rest * align + kappa * rest * (us_g + gs_u) + kappa * kappa * us_u
    )
    blend = align_next / align
    lead = rest + blend
    curve_next = (
        lead * lead * curve + lead * kappa * (us_p1 + q1_u) + kappa * kappa * us_p2
    )
    step_next = align_next / curve_next

    def column(value):
        return value[:, None]

    step, kappa, lead, step_next = map(column, (step, kappa, lead, step_next))
    direction = lead * g + kappa * u
    shadow_direction = lead * gs + kappa * us
    solution = step * g + step_next * direction
    shadow_solution = step * gs + step_next * shadow_direction
    residual = g - step * p1 - step_next * (lead * p1 + kappa * p2)
    shadow_residual = gs - step * q1 - step_next * (lead * q1 + kappa * q2)
    return (solution, shadow_solution, residual, shadow_residual)


def solution(mesh):
    return jax.shard_map(
        on_device,
        mesh=mesh,
        in_specs=(P("row", "col"), P(None, "col"), P(None, "col"), P(None, "col")),
        out_specs=(P(None, "col"), P(None, "col"), P(None, "col"), P(None, "col")),
        check_vma=False,
    )
```
